128 devices in a mesh: span: 8 (over y, core), chord: 16 (over z, x).
Axes of the slice: x: 4, y: 4, z: 4, core: 2. Of those that a mesh axis runs over, the one named last changes fastest.
Arguments:
- adjoint_source: float32 [6, 125, 32768], P(None, None, ('span', 'chord')), may hold values from -18 to 18
- degrees: int32 [32768], P(('span', 'chord')), may hold values from 1 to 4
- time_shift: float32 [32768], P(('span', 'chord')), may hold values from 1.5 to 4
- flux_jacobian: float32 [3, 6, 6, 32768], P(None, None, None, ('span', 'chord')), may hold values from -1.75 to 1.75
- block_inverse: float32 [6, 6, 32768], P(None, None, ('span', 'chord')), may hold values from -0.05 to 0.7, as said below
- dissipation: float32 [6, 6], replicated, may hold values from -0.45 to 0.7
- convection: float32 [6, 6], replicated, may hold values from -0.9 to 0.9
- face_weight: float32 [65536], P(('span', 'chord')), may hold values from 0.5 to 2
- face_elements: int32 [2, 65536], P(None, ('span', 'chord')), may hold values from 0 to 255
- face_numbers: int32 [2, 65536], P(None, ('span', 'chord')), may hold values from 0 to 5
- boundary_elements: int32 [4, 16384], P(None, ('span', 'chord')), may hold values from 0 to 255
- boundary_numbers: int32 [4, 16384], P(None, ('span', 'chord')), may hold values from 0 to 5
Outputs:
- adjoint: float32 [6, 125, 32768], P(None, None, ('span', 'chord'))
The draws below stay inside these ranges and needn't reach their ends.
Inputs may be any that keep to these rules, and one draw needn't show every extreme that they name: `block_inverse`: diagonally dominant per element.
All inputs are finite; a program needn't handle non-finite values.
Results may differ from the reference program's by a relative error of at most 0.0024.
Values sent between devices are 32-bit elements; how exact they have to be, the bound alone decides.
A program may use at most 128 MiB of HBM per device.

```python
import math
import jax
import jax.numpy as jnp
from jax import lax

NV = 6
MODES = 125
E_DEV = 256
FS = 128
ITERS = 4
IF_DEV = 512
ELEMS = 32768
IFACES = 65536
BFACES = 16384
N_SPAN = 8
N_CHORD = 16
DEVICES = 128


def draw_adjoint_source(key, part):
    key = jax.random.fold_in(key, 11)
    ramp = 1.0 + 2.0 * jnp.arange(ELEMS, dtype=jnp.float32) / ELEMS
    base = jnp.clip(jax.random.normal(key, (NV, MODES, ELEMS), jnp.float32), -5.0, 5.0)
    return (base * ramp[None, None, :]).astype(jnp.float32)


def draw_block_inverse(key, part):
    key = jax.random.fold_in(key, 12)
    diag_key, off_key = jax.random.split(key)
    identity = jnp.eye(NV, dtype=jnp.float32)[:, :, None]
    diagonal = jax.random.uniform(diag_key, (1, NV, ELEMS), jnp.float32, 0.25, 0.6)
    offdiag = 0.02 * jnp.clip(jax.random.normal(off_key, (NV, NV, ELEMS), jnp.float32), -2.4, 2.4)
    return (identity * diagonal + (1.0 - identity) * offdiag).astype(jnp.float32)


def draw_dissipation(key, part):
    key = jax.random.fold_in(key, 13)
    diag_key, off_key = jax.random.split(key)
    identity = jnp.eye(NV, dtype=jnp.float32)
    diagonal = jax.random.uniform(diag_key, (NV,), jnp.float32, 0.3, 0.7)
    offdiag = 0.08 * jnp.clip(jax.random.normal(off_key, (NV, NV), jnp.float32), -5.0, 5.0)
    return (identity * diagonal[None, :] + (1.0 - identity) * offdiag).astype(jnp.float32)


def with_ends(drawn, own_key, low, largest):
    place = [jax.random.randint(jax.random.fold_in(own_key, axis), (), 0, length) for axis, length in enumerate(drawn.shape)]
    longest = drawn.shape.index(max(drawn.shape))
    beside = place[:longest] + [(place[longest] + 1) % drawn.shape[longest]] + place[longest + 1:]
    return drawn.at[tuple(place)].set(low).at[tuple(beside)].set(largest)


def block_levels(own_key, dims, pieces, low, top_value):
    loudness, own = 1.0, jax.random.fold_in(own_key, 6)
    for dim, parts in pieces:
        steps = jnp.exp(jax.random.uniform(jax.random.fold_in(own, dim), (parts,), jnp.float32, low / len(pieces), top_value / len(pieces)))
        loudness = loudness * jnp.repeat(steps, dims[dim] // parts).reshape([-1 if axis == dim else 1 for axis in range(len(dims))])
    return loudness


def centred(key, shape, spread, limit, shards=(), kind=jnp.bfloat16):
    values = spread * jax.random.normal(key, shape, jnp.float32)
    if shards:
        values = values * block_levels(key, shape, shards, -0.22, 0.18)
    return jnp.clip(values, -limit, limit).astype(kind)


def setup_inputs(seed: int = 0) -> dict:
    arg_keys = jax.random.split(jax.random.key(seed), 13)
    adjoint_source = draw_adjoint_source(jax.random.fold_in(arg_keys[12], 71), 0)
    degrees = with_ends(jax.random.randint(arg_keys[1], (ELEMS,), 1, 5), jax.random.fold_in(arg_keys[1], 1), 1, 4).astype(jnp.int32)
    time_shift = jnp.clip(jnp.exp(math.log(4.0) - 0.98082925 * jax.random.uniform(arg_keys[2], (ELEMS,), jnp.float32) ** block_levels(arg_keys[2], (ELEMS,), ((0, 128),), -0.2, 0.2)), 1.5, 4.0)
    flux_jacobian = centred(arg_keys[3], (3, NV, NV, ELEMS), (2 * NV) ** -0.5, 1.75, ((3, 128),), jnp.float32)
    block_inverse = draw_block_inverse(jax.random.fold_in(arg_keys[12], 71), 0)
    dissipation = draw_dissipation(jax.random.fold_in(arg_keys[12], 71), 0)
    convection = centred(arg_keys[6], (NV, NV), 0.15, 0.9, (), jnp.float32)
    face_weight = jnp.clip(jnp.exp(math.log(2.0) - 1.3862944 * jax.random.uniform(arg_keys[7], (IFACES,), jnp.float32) ** block_levels(arg_keys[7], (IFACES,), ((0, 128),), -0.2, 0.2)), 0.5, 2.0)
    face_elements = with_ends(jax.random.randint(arg_keys[8], (2, IFACES), 0, E_DEV), jax.random.fold_in(arg_keys[8], 1), 0, E_DEV - 1).astype(jnp.int32)
    face_numbers = with_ends(jax.random.randint(arg_keys[9], (2, IFACES), 0, 6), jax.random.fold_in(arg_keys[9], 1), 0, 5).astype(jnp.int32)
    boundary_elements = with_ends(jax.random.randint(arg_keys[10], (4, BFACES), 0, E_DEV), jax.random.fold_in(arg_keys[10], 1), 0, E_DEV - 1).astype(jnp.int32)
    boundary_numbers = with_ends(jax.random.randint(arg_keys[11], (4, BFACES), 0, 6), jax.random.fold_in(arg_keys[11], 1), 0, 5).astype(jnp.int32)
    return dict(adjoint_source=adjoint_source, degrees=degrees, time_shift=time_shift, flux_jacobian=flux_jacobian, block_inverse=block_inverse, dissipation=dissipation, convection=convection, face_weight=face_weight, face_elements=face_elements, face_numbers=face_numbers, boundary_elements=boundary_elements, boundary_numbers=boundary_numbers)


HIGHEST = lax.Precision.HIGHEST

def tables():
    index = jnp.arange(5, dtype=jnp.int32)
    row_index = index[:, None]
    col_index = index[None, :]
    deriv = jnp.where((col_index > row_index) & ((col_index - row_index) % 2 == 1), 0.2 * (2 * row_index + 1).astype(jnp.float32), 0.0).astype(jnp.float32)
    alternate = jnp.where(index % 2 == 0, 1.0, -1.0).astype(jnp.float32)
    trace_table = 0.5 * jnp.stack([alternate, jnp.ones((5,), jnp.float32)])
    return (deriv, trace_table)

def active_modes(degrees):
    modes = jnp.arange(125, dtype=jnp.int32)
    highest = jnp.maximum(jnp.maximum(modes // 25, modes // 5 % 5), modes % 5)
    return (highest[:, None] <= degrees[None, :]).astype(jnp.float32)

def volume_term(field, time_shift, flux_jacobian, deriv):
    nvar, modes, count = field.shape
    cube = field.reshape(nvar, 5, 5, 5, count)
    result = time_shift[None, None, :] * field
    grads = [jnp.einsum('ji,bikle->bjkle', deriv, cube, precision=HIGHEST), jnp.einsum('ji,bkile->bkjle', deriv, cube, precision=HIGHEST), jnp.einsum('ji,bklie->bklje', deriv, cube, precision=HIGHEST)]
    for direction in range(3):
        result = result + jnp.einsum('abe,bme->ame', flux_jacobian[direction], grads[direction].reshape(nvar, modes, count), precision=HIGHEST)
    return result

def face_traces(field, trace_table):
    nvar, modes, count = field.shape
    cube = field.reshape(nvar, 5, 5, 5, count)
    first = jnp.einsum('si,bijke->bjkse', trace_table, cube, precision=HIGHEST).reshape(nvar, 25, 2, count)
    second = jnp.einsum('sj,bijke->bikse', trace_table, cube, precision=HIGHEST).reshape(nvar, 25, 2, count)
    third = jnp.einsum('sk,bijke->bijse', trace_table, cube, precision=HIGHEST).reshape(nvar, 25, 2, count)
    return jnp.concatenate([first, second, third], axis=2)

def lift_faces(faces, trace_table):
    nvar = faces.shape[0]
    count = faces.shape[3]
    grid = faces.reshape(nvar, 5, 5, 6, count)
    result = jnp.einsum('si,bjkse->bijke', trace_table, grid[:, :, :, 0:2, :], precision=HIGHEST)
    result = result + jnp.einsum('sj,bikse->bijke', trace_table, grid[:, :, :, 2:4, :], precision=HIGHEST)
    result = result + jnp.einsum('sk,bijse->bijke', trace_table, grid[:, :, :, 4:6, :], precision=HIGHEST)
    return result.reshape(nvar, 125, count)

def face_flux(own_trace, other_trace, dissipation, convection, sign):
    nvar = dissipation.shape[0]
    difference = (own_trace - other_trace).reshape(nvar, 25, -1)
    combined = (own_trace + other_trace).reshape(nvar, 25, -1)
    result = jnp.einsum('xy,ymf->xmf', dissipation, difference, precision=HIGHEST)
    result = result + sign * jnp.einsum('xy,ymf->xmf', convection, combined, precision=HIGHEST)
    return result.reshape(own_trace.shape)

def reference(adjoint_source, degrees, time_shift, flux_jacobian, block_inverse, dissipation, convection, face_weight, face_elements, face_numbers, boundary_elements, boundary_numbers):
    deriv, trace_table = tables()
    nvar = adjoint_source.shape[0]
    rows = nvar * 25
    active = active_modes(degrees)
    inner_device = jnp.arange(IFACES, dtype=jnp.int32) // IF_DEV
    inner_cols = inner_device[None, :] * (6 * E_DEV) + face_numbers * E_DEV + face_elements
    side_device = jnp.arange(BFACES, dtype=jnp.int32) // FS
    side_cols = side_device[None, :] * (6 * E_DEV) + boundary_numbers * E_DEV + boundary_elements

    def operator(field):
        traces = face_traces(field, trace_table).reshape(rows, 6, DEVICES, E_DEV)
        flat = traces.transpose(0, 2, 1, 3).reshape(rows, DEVICES * 6 * E_DEV)
        left_trace = flat[:, inner_cols[0]]
        right_trace = flat[:, inner_cols[1]]
        term = face_flux(left_trace, right_trace, dissipation, convection, 1.0) * face_weight[None, :]
        gathered = jnp.zeros_like(flat).at[:, inner_cols[0]].add(term).at[:, inner_cols[1]].add(-term)
        sides = flat[:, side_cols.reshape(-1)].reshape(rows, 4, N_SPAN, N_CHORD, FS)
        zero_span = jnp.zeros((rows, 1, N_CHORD, FS), jnp.float32)
        zero_chord = jnp.zeros((rows, N_SPAN, 1, FS), jnp.float32)
        others = [jnp.concatenate([zero_span, sides[:, 1, :-1]], axis=1), jnp.concatenate([sides[:, 0, 1:], zero_span], axis=1), jnp.concatenate([zero_chord, sides[:, 3, :, :-1]], axis=2), jnp.concatenate([sides[:, 2, :, 1:], zero_chord], axis=2)]
        signs = [-1.0, 1.0, -1.0, 1.0]
        for side in range(4):
            part = face_flux(sides[:, side].reshape(rows, -1), others[side].reshape(rows, -1), dissipation, convection, signs[side])
            gathered = gathered.at[:, side_cols[side]].add(part)
        faces = gathered.reshape(rows, DEVICES, 6, E_DEV).transpose(0, 2, 1, 3).reshape(nvar, 25, 6, ELEMS)
        result = volume_term(field, time_shift, flux_jacobian, deriv) + lift_faces(faces, trace_table)
        return result * active[None]

    def precondition(field):
        return active[None] * jnp.einsum('abe,bme->ame', block_inverse, field, precision=HIGHEST)
    source = active[None] * adjoint_source
    beta = jnp.sqrt(jnp.sum(source * source))
    basis = [source / beta]
    directions = []
    hess = jnp.zeros((ITERS + 1, ITERS), jnp.float32)
    for step in range(ITERS):
        direction = precondition(basis[step])
        directions.append(direction)
        image = operator(direction)
        products = [jnp.sum(vector * image) for vector in basis]
        for position in range(step + 1):
            image = image - products[position] * basis[position]
            hess = hess.at[position, step].set(products[position])
        length = jnp.sqrt(jnp.sum(image * image))
        hess = hess.at[step + 1, step].set(length)
        basis.append(image / length)
    normal = jnp.dot(hess.T, hess, precision=HIGHEST)
    factor = jnp.linalg.cholesky(normal)
    coeffs = jax.scipy.linalg.cho_solve((factor, True), beta * hess[0])
    adjoint = coeffs[0] * directions[0]
    for step in range(1, ITERS):
        adjoint = adjoint + coeffs[step] * directions[step]
    return adjoint
```

```python
import functools

import jax
import jax.numpy as jnp
import numpy as np
from jax import lax
from jax.experimental import pallas as pl
from jax.experimental.pallas import tpu as pltpu
from jax.sharding import PartitionSpec as P

ITERS = 4
NV = 6
E = 256
IF = 512
FS = 128
NF = 6
ROWS = 160
SEND = 152
COLS = NF * E
SLOTS = 2 * IF + 4 * FS
SHIFT = 1.5
MESH = pl.DeviceIdType.MESH
BF = jnp.bfloat16
F32 = jnp.float32


def face_row(face, t):
    return face * 24 + t if t < 24 else 144 + face


def constants():
    mode_mat = np.zeros((ROWS + 384, 128), np.float32)
    lift = np.zeros((128, ROWS), np.float32)
    sign = [1.0, -1.0, 1.0, -1.0, 1.0]
    for i in range(5):
        for j in range(5):
            for k in range(5):
                m = 25 * i + 5 * j + k
                idx = (i, j, k)
                rest = (5 * j + k, 5 * i + k, 5 * i + j)
                step = (25, 5, 1)
                for d in range(3):
                    for end in range(2):
                        r = face_row(2 * d + end, rest[d])
                        value = 0.5 * (sign[idx[d]] if end == 0 else 1.0)
                        mode_mat[r, m] = value
                        lift[m, r] = value
                    for low in range(idx[d]):
                        if (idx[d] - low) % 2 == 1:
                            out = m - step[d] * (idx[d] - low)
                            mode_mat[ROWS + 128 * d + out, m] = 2 * low + 1
    highest = np.full((128, 128), 99, np.int32)
    for m in range(125):
        highest[m] = max(m // 25, m // 5 % 5, m % 5)
    return (
        jnp.asarray(np.concatenate([mode_mat, mode_mat], axis=1), BF),
        jnp.asarray(np.concatenate([lift, lift], axis=1), BF),
        jnp.asarray(highest),
    )


def split(x):
    hi = x.astype(BF)
    return hi, (x - hi.astype(F32)).astype(BF)


def dot(a, b):
    return jnp.dot(a, b, preferred_element_type=F32)


def dot_t(a, b):
    return lax.dot_general(a, b, (((1,), (1,)), ((), ())), preferred_element_type=F32)


def kernel(
    n_span,
    n_chord,
    src,
    degrees,
    time_shift,
    jac,
    binv,
    diss,
    conv,
    weight,
    face_el,
    face_no,
    side_el,
    side_no,
    mode_mat,
    lift_mat,
    highest,
    out,
    active,
    jac2,
    select,
    mix,
    us,
    zs,
    modes,
    grads,
    flat,
    flat_b,
    own,
    interior,
    uv_b,
    term_b,
    gathered,
    faces,
    sends,
    recvs,
    gram,
    red1,
    red2,
    send_sem,
    recv_sem,
    r1_send,
    r1_recv,
    r2_send,
    r2_recv,
):
    span = lax.axis_index("span")
    chord = lax.axis_index("chord")

    barrier = pltpu.get_barrier_semaphore()
    for i in range(1, n_span):
        pl.semaphore_signal(
            barrier, inc=1, device_id=(lax.rem(span + i, n_span), chord), device_id_type=MESH
        )
    for i in range(1, n_chord):
        pl.semaphore_signal(
            barrier, inc=1, device_id=(span, lax.rem(chord + i, n_chord)), device_id_type=MESH
        )

    has = (span > 0, span < n_span - 1, chord > 0, chord < n_chord - 1)
    targets = ((span - 1, chord), (span + 1, chord), (span, chord - 1), (span, chord + 1))

    act = (highest[:, 0:1] <= degrees[...].reshape(1, E)).astype(F32)
    active[...] = act
    for b in range(NV):
        us[0, b, 125:128, :] = jnp.zeros((3, E), F32)
        us[0, b, 0:125, :] = src[b] * act[0:125]
    jac2[...] = jac[...] * 0.2

    cols_in = face_no[...] * E + face_el[...]
    cols_sd = side_no[...] * E + side_el[...]
    left = cols_in[0:1, :]
    right = cols_in[1:2, :]
    row16 = lax.broadcasted_iota(jnp.int32, (16, FS), 0)

    def build(c, carry):
        base = pl.multiple_of(c * 16, 16)
        rows = row16 + base
        for q in range(4):
            l = (rows == left[:, q * FS : (q + 1) * FS]).astype(F32)
            r = (rows == right[:, q * FS : (q + 1) * FS]).astype(F32)
            s = (rows == cols_sd[q : q + 1, :]).astype(F32)
            select[pl.ds(base, 16), q * FS : (q + 1) * FS] = (l - r).astype(BF)
            select[pl.ds(base, 16), IF + q * FS : IF + (q + 1) * FS] = (l + r).astype(BF)
            select[pl.ds(base, 16), 2 * IF + q * FS : 2 * IF + (q + 1) * FS] = s.astype(BF)
        return carry

    lax.fori_loop(0, COLS // 16, build, 0)

    r24 = lax.broadcasted_iota(jnp.int32, (24, ROWS), 0)
    c24 = lax.broadcasted_iota(jnp.int32, (24, ROWS), 1)
    r16 = lax.broadcasted_iota(jnp.int32, (16, ROWS), 0)
    c16 = lax.broadcasted_iota(jnp.int32, (16, ROWS), 1)
    mixed = []
    for mat in (diss, conv):
        parts = []
        for x in range(NV):
            acc = jnp.zeros((24, ROWS), F32)
            for y in range(NV):
                acc = acc + jnp.where(c24 == r24 + y * 24, mat[x, y], 0.0)
            parts.append(acc)
        acc = jnp.zeros((16, ROWS), F32)
        for x in range(NV):
            for y in range(NV):
                acc = acc + jnp.where((r16 == x) & (c16 == 144 + y), mat[x, y], 0.0)
        parts.append(acc)
        mixed.append(jnp.concatenate(parts, axis=0))
    mixed = jnp.concatenate(mixed, axis=1)
    mix_hi, mix_lo = split(mixed)
    mix[:, 0 : 2 * ROWS] = mix_hi
    mix[:, 2 * ROWS : 4 * ROWS] = mix_hi
    mix[:, 4 * ROWS : 6 * ROWS] = mix_lo

    flat[...] = jnp.zeros_like(flat)
    faces[...] = jnp.zeros_like(faces)
    for s in range(4):

        @pl.when(jnp.logical_not(has[s]))
        def _(s=s):
            for k in range(ITERS):
                recvs[k, s] = jnp.zeros((SEND, FS), F32)

    pl.semaphore_wait(barrier, n_span + n_chord - 2)

    def side_copy(step, s):
        return pltpu.make_async_remote_copy(
            src_ref=sends.at[step, s],
            dst_ref=recvs.at[step, s ^ 1],
            send_sem=send_sem.at[step, s],
            recv_sem=recv_sem.at[step, s ^ 1],
            device_id=targets[s],
            device_id_type=MESH,
        )

    def mix_terms(difference, total):
        d_hi, d_lo = split(difference)
        t_hi, t_lo = split(total)
        n = difference.shape[1]
        for k, part in enumerate((d_hi, t_hi, d_lo, t_lo, d_hi, t_hi)):
            uv_b[k * ROWS : (k + 1) * ROWS, 0:n] = part
        return dot(mix[...], uv_b[:, 0:n])

    def one_step(step, carry):
        for lt in range(2):
            lanes = slice(lt * 128, (lt + 1) * 128)
            for a0 in range(0, NV, 2):
                acc = [None, None]
                for b in range(NV):
                    u = us[step, b, :, lanes]
                    for p in range(2):
                        t = binv[a0 + p, b : b + 1, lanes] * u
                        acc[p] = t if acc[p] is None else acc[p] + t
                for p in range(2):
                    zs[step, a0 + p, :, lanes] = acc[p]
                    hi, lo = split(acc[p])
                    modes[a0 + p, 0:128, lanes] = hi
                    modes[a0 + p, 128:256, lanes] = lo
        for b in range(NV):
            t = dot(mode_mat[0:ROWS, :], modes[b])
            for f in range(NF):
                flat[b * 24 : (b + 1) * 24, f * E : (f + 1) * E] = t[f * 24 : (f + 1) * 24]
                flat[144 + b : 145 + b, f * E : (f + 1) * E] = t[144 + f : 145 + f]
        for f in range(NF):
            hi, lo = split(flat[:, f * E : (f + 1) * E])
            flat_b[0:ROWS, f * E : (f + 1) * E] = hi
            flat_b[ROWS : 2 * ROWS, f * E : (f + 1) * E] = lo
        t = dot(flat_b[...], select[:, 2 * IF :])
        own[...] = t[0:ROWS] + t[ROWS:]
        for s in range(4):
            sends[step, s] = own[0:SEND, s * FS : (s + 1) * FS]

            @pl.when(has[s])
            def _(s=s):
                side_copy(step, s).start()

        for b in range(NV):
            grads[b] = dot(mode_mat[ROWS:, :], modes[b])
        for q in range(2):
            t = dot(flat_b[...], select[:, q * IF : (q + 1) * IF])
            interior[q] = t[0:ROWS] + t[ROWS:]
        term = mix_terms(interior[0], interior[1]) * weight[...].reshape(1, IF)
        hi, lo = split(term)
        term_b[0:ROWS] = hi
        term_b[ROWS:] = lo
        for f in range(NF):
            t = dot_t(term_b[...], select[f * E : (f + 1) * E, 0:IF])
            gathered[:, f * E : (f + 1) * E] = t[0:ROWS] + t[ROWS:]
        for lt in range(2):
            lanes = slice(lt * 128, (lt + 1) * 128)
            shift = time_shift[...].reshape(1, E)[:, lanes]
            for a0 in range(0, NV, 2):
                acc = [shift * zs[step, a0 + p, :, lanes] for p in range(2)]
                for d in range(3):
                    for b in range(NV):
                        g = grads[b, d * 128 : (d + 1) * 128, lanes]
                        for p in range(2):
                            acc[p] = acc[p] + jac2[d, a0 + p, b : b + 1, lanes] * g
                for p in range(2):
                    us[step + 1, a0 + p, :, lanes] = acc[p]
        for s in range(4):

            @pl.when(has[s])
            def _(s=s):
                side_copy(step, s ^ 1).wait_recv()

        diffs, sums = [], []
        for s in range(4):
            mine = own[:, s * FS : (s + 1) * FS]
            other = jnp.concatenate([recvs[step, s], jnp.zeros((ROWS - SEND, FS), F32)], axis=0)
            diffs.append(mine - other)
            sums.append(mine + other if s % 2 == 1 else -(mine + other))
        term = mix_terms(jnp.concatenate(diffs, axis=1), jnp.concatenate(sums, axis=1))
        hi, lo = split(term)
        term_b[0:ROWS] = hi
        term_b[ROWS:] = lo
        for f in range(NF):
            t = dot_t(term_b[...], select[f * E : (f + 1) * E, 2 * IF :])
            t = gathered[:, f * E : (f + 1) * E] + (t[0:ROWS] + t[ROWS:])
            for b in range(NV):
                faces[b, f * 24 : (f + 1) * 24, :] = t[b * 24 : (b + 1) * 24]
                faces[b, 144 + f : 145 + f, :] = t[144 + b : 145 + b]
        for b in range(NV):
            hi, lo = split(faces[b])
            t = dot(lift_mat[...], jnp.concatenate([hi, lo], axis=0))
            us[step + 1, b] = (us[step + 1, b] + t) * active[...] - SHIFT * us[step, b]
        for s in range(4):

            @pl.when(has[s])
            def _(s=s):
                side_copy(step, s).wait_send()

        return carry

    lax.fori_loop(0, ITERS, one_step, 0)

    pairs = [(i, j) for i in range(ITERS + 1) for j in range(i, ITERS + 1)]

    def products(c, accs):
        accs = list(accs)
        base = pl.multiple_of(c * 8, 8)
        for b in range(NV):
            for lt in range(2):
                lanes = slice(lt * 128, (lt + 1) * 128)
                u = [us[k, b, pl.ds(base, 8), lanes] for k in range(ITERS + 1)]
                for n, (i, j) in enumerate(pairs):
                    accs[n] = accs[n] + u[i] * u[j]
        return tuple(accs)

    accs = lax.fori_loop(0, 16, products, tuple(jnp.zeros((8, 128), F32) for _ in pairs))
    rows = [jnp.sum(x, axis=0, keepdims=True) for x in accs]
    rows.append(jnp.zeros((1, 128), F32))
    x = jnp.concatenate(rows, axis=0)
    for amount in (64, 32, 16, 8):
        x = x + pltpu.roll(x, amount, 1)
    row = lax.broadcasted_iota(jnp.int32, (16, 128), 0)
    lane = lax.broadcasted_iota(jnp.int32, (16, 128), 1)
    x = jnp.sum(jnp.where((lane >= row * 8) & (lane < row * 8 + 8), x, 0.0), axis=0, keepdims=True)
    gram[0] = jnp.broadcast_to(x, (8, 128))

    def r1_copy(i):
        return pltpu.make_async_remote_copy(
            src_ref=gram.at[0],
            dst_ref=red1.at[i],
            send_sem=r1_send.at[i],
            recv_sem=r1_recv.at[i],
            device_id=(lax.rem(span + i, n_span), chord),
            device_id_type=MESH,
        )

    def r2_copy(i):
        return pltpu.make_async_remote_copy(
            src_ref=gram.at[1],
            dst_ref=red2.at[i],
            send_sem=r2_send.at[i],
            recv_sem=r2_recv.at[i],
            device_id=(span, lax.rem(chord + i, n_chord)),
            device_id_type=MESH,
        )

    for i in range(1, n_span):
        r1_copy(i).start()
    total = gram[0]
    for i in range(1, n_span):
        r1_copy(i).wait_recv()
        total = total + red1[i]
    gram[1] = total
    for i in range(1, n_chord):
        r2_copy(i).start()
    total = gram[1]
    for i in range(1, n_chord):
        r2_copy(i).wait_recv()
        total = total + red2[i]
    for amount in (4, 2, 1):
        total = total + pltpu.roll(total, 128 - amount, 1)

    g = {}
    for n, (i, j) in enumerate(pairs):
        g[i, j] = g[j, i] = jnp.broadcast_to(total[:, 8 * n : 8 * n + 1], (8, 128))
    half = [[SHIFT * g[i, j] + g[i, j + 1] for j in range(ITERS)] for i in range(ITERS + 1)]
    normal = [
        [SHIFT * half[i][j] + half[i + 1][j] for j in range(ITERS)] for i in range(ITERS)
    ]
    rhs = [half[0][j] for j in range(ITERS)]
    low = [[None] * ITERS for _ in range(ITERS)]
    pivot, inv = [], []
    for j in range(ITERS):
        d = normal[j][j]
        for k in range(j):
            d = d - low[j][k] * low[j][k] * pivot[k]
        pivot.append(d)
        usable = d > 1e-6 * normal[j][j]
        inv.append(jnp.where(usable, 1.0 / jnp.where(usable, d, 1.0), 0.0))
        for i in range(j + 1, ITERS):
            v = normal[i][j]
            for k in range(j):
                v = v - low[i][k] * low[j][k] * pivot[k]
            low[i][j] = v * inv[j]
    y = []
    for i in range(ITERS):
        v = rhs[i]
        for k in range(i):
            v = v - low[i][k] * y[k]
        y.append(v)
    coeffs = [y[i] * inv[i] for i in range(ITERS)]
    for i in reversed(range(ITERS)):
        for k in range(i + 1, ITERS):
            coeffs[i] = coeffs[i] - low[k][i] * coeffs[k]
    coeffs = [c[0:1, :] for c in coeffs]
    for b in range(NV):
        for lt in range(2):
            lanes = slice(lt * 128, (lt + 1) * 128)
            x = coeffs[0] * zs[0, b, 0:125, lanes]
            for k in range(1, ITERS):
                x = x + coeffs[k] * zs[k, b, 0:125, lanes]
            out[b, :, lanes] = x

    for i in range(1, n_span):
        r1_copy(i).wait_send()
    for i in range(1, n_chord):
        r2_copy(i).wait_send()


def local(n_span, n_chord, *args):
    vmem = pl.BlockSpec(memory_space=pltpu.VMEM)
    smem = pl.BlockSpec(memory_space=pltpu.SMEM)
    specs = [vmem] * 15
    specs[5] = specs[6] = smem
    return pl.pallas_call(
        functools.partial(kernel, n_span, n_chord),
        out_shape=jax.ShapeDtypeStruct((NV, 125, E), F32),
        in_specs=specs,
        out_specs=vmem,
        scratch_shapes=[
            pltpu.VMEM((128, E), F32),
            pltpu.VMEM((3, NV, NV, E), F32),
            pltpu.VMEM((COLS, SLOTS), BF),
            pltpu.VMEM((ROWS, 6 * ROWS), BF),
            pltpu.VMEM((ITERS + 1, NV, 128, E), F32),
            pltpu.VMEM((ITERS, NV, 128, E), F32),
            pltpu.VMEM((NV, 256, E), BF),
            pltpu.VMEM((NV, 384, E), F32),
            pltpu.VMEM((ROWS, COLS), F32),
            pltpu.VMEM((2 * ROWS, COLS), BF),
            pltpu.VMEM((ROWS, 4 * FS), F32),
            pltpu.VMEM((2, ROWS, IF), F32),
            pltpu.VMEM((6 * ROWS, IF), BF),
            pltpu.VMEM((2 * ROWS, IF), BF),
            pltpu.VMEM((ROWS, COLS), F32),
            pltpu.VMEM((NV, ROWS, E), F32),
            pltpu.VMEM((ITERS, 4, SEND, FS), F32),
            pltpu.VMEM((ITERS, 4, SEND, FS), F32),
            pltpu.VMEM((2, 8, 128), F32),
            pltpu.VMEM((n_span, 8, 128), F32),
            pltpu.VMEM((n_chord, 8, 128), F32),
            pltpu.SemaphoreType.DMA((ITERS, 4)),
            pltpu.SemaphoreType.DMA((ITERS, 4)),
            pltpu.SemaphoreType.DMA((n_span,)),
            pltpu.SemaphoreType.DMA((n_span,)),
            pltpu.SemaphoreType.DMA((n_chord,)),
            pltpu.SemaphoreType.DMA((n_chord,)),
        ],
        compiler_params=pltpu.CompilerParams(
            collective_id=0, has_side_effects=True, vmem_limit_bytes=48 * 1024 * 1024
        ),
    )(*args, *constants())


def solution(mesh):
    placed = (
        P(None, None, ("span", "chord")),
        P(("span", "chord")),
        P(("span", "chord")),
        P(None, None, None, ("span", "chord")),
        P(None, None, ("span", "chord")),
        P(),
        P(),
        P(("span", "chord")),
        P(None, ("span", "chord")),
        P(None, ("span", "chord")),
        P(None, ("span", "chord")),
        P(None, ("span", "chord")),
    )
    return jax.shard_map(
        functools.partial(local, mesh.shape["span"], mesh.shape["chord"]),
        mesh=mesh,
        in_specs=placed,
        out_specs=P(None, None, ("span", "chord")),
        check_vma=False,
    )
```

```python
import functools

import jax
import jax.numpy as jnp
import numpy as np
from jax import lax
from jax.experimental import pallas as pl
from jax.experimental.pallas import tpu as pltpu
from jax.sharding import PartitionSpec as P

ITERS = 4
NV = 6
E = 256
IF = 512
FS = 128
NF = 6
ROWS = 160
SEND = 152
COLS = NF * E
SLOTS = 2 * IF + 4 * FS
SHIFT = 1.5
LOAD_ORDER = (8, 9, 10, 11, 0, 1, 4, 12, 3, 5, 6, 7, 2, 13)
MESH = pl.DeviceIdType.MESH
BF = jnp.bfloat16
F32 = jnp.float32


def face_row(face, t):
    return face * 24 + t if t < 24 else 144 + face


def constants():
    mode_mat = np.zeros((ROWS + 384, 128), np.float32)
    lift = np.zeros((128, ROWS), np.float32)
    sign = [1.0, -1.0, 1.0, -1.0, 1.0]
    for i in range(5):
        for j in range(5):
            for k in range(5):
                m = 25 * i + 5 * j + k
                idx = (i, j, k)
                rest = (5 * j + k, 5 * i + k, 5 * i + j)
                step = (25, 5, 1)
                for d in range(3):
                    for end in range(2):
                        r = face_row(2 * d + end, rest[d])
                        value = 0.5 * (sign[idx[d]] if end == 0 else 1.0)
                        mode_mat[r, m] = value
                        lift[m, r] = value
                    for low in range(idx[d]):
                        if (idx[d] - low) % 2 == 1:
                            out = m - step[d] * (idx[d] - low)
                            mode_mat[ROWS + 128 * d + out, m] = 2 * low + 1
    return (
        jnp.asarray(mode_mat),
        jnp.asarray(np.concatenate([lift, lift], axis=1)),
    )


def split(x):
    hi = x.astype(BF)
    return hi, (x - hi.astype(F32)).astype(BF)


def dot(a, b):
    return jnp.dot(a, b, preferred_element_type=F32)


def dot_t(a, b):
    return lax.dot_general(a, b, (((1,), (1,)), ((), ())), preferred_element_type=F32)


def kernel(
    n_span,
    n_chord,
    *refs,
):
    operands, (out,), refs = refs[:14], refs[14:15], refs[15:]
    held, load_sem, refs = refs[:14], refs[14], refs[15:]
    (
        src,
        degrees,
        time_shift,
        jac,
        binv,
        diss,
        conv,
        weight,
        face_el,
        face_no,
        side_el,
        side_no,
        mode_in,
        lift_in,
    ) = held
    (
        mode_mat,
        lift_mat,
        active,
        jac2,
        select,
        mix,
        us,
        zs,
        modes,
        grads,
        flat,
        flat_b,
        own,
        interior,
        uv_b,
        term_b,
        gathered,
        faces,
        sends,
        recvs,
        gram,
        red1,
        red2,
        send_sem,
        recv_sem,
        r1_send,
        r1_recv,
        r2_send,
        r2_recv,
    ) = refs
    loads = [pltpu.make_async_copy(a, b, load_sem.at[k]) for k, (a, b) in enumerate(zip(operands, held))]
    for k in LOAD_ORDER:
        loads[k].start()

    def arrived(*which):
        for k in which:
            loads[k].wait()

    span = lax.axis_index("span")
    chord = lax.axis_index("chord")

    barrier = pltpu.get_barrier_semaphore()
    for i in range(1, n_span):
        pl.semaphore_signal(
            barrier, inc=1, device_id=(lax.rem(span + i, n_span), chord), device_id_type=MESH
        )
    for i in range(1, n_chord):
        pl.semaphore_signal(
            barrier, inc=1, device_id=(span, lax.rem(chord + i, n_chord)), device_id_type=MESH
        )

    has = (span > 0, span < n_span - 1, chord > 0, chord < n_chord - 1)
    targets = ((span - 1, chord), (span + 1, chord), (span, chord - 1), (span, chord + 1))

    arrived(8, 9, 10, 11)
    cols_in = face_no[...] * E + face_el[...]
    cols_sd = side_no[...] * E + side_el[...]
    left = cols_in[0:1, :]
    right = cols_in[1:2, :]
    row16 = lax.broadcasted_iota(jnp.int32, (16, FS), 0)

    def build(c, carry):
        base = pl.multiple_of(c * 16, 16)
        rows = row16 + base
        for q in range(4):
            l = (rows == left[:, q * FS : (q + 1) * FS]).astype(F32)
            r = (rows == right[:, q * FS : (q + 1) * FS]).astype(F32)
            s = (rows == cols_sd[q : q + 1, :]).astype(F32)
            select[pl.ds(base, 16), q * FS : (q + 1) * FS] = (l - r).astype(BF)
            select[pl.ds(base, 16), IF + q * FS : IF + (q + 1) * FS] = (l + r).astype(BF)
            select[pl.ds(base, 16), 2 * IF + q * FS : 2 * IF + (q + 1) * FS] = s.astype(BF)
        return carry

    lax.fori_loop(0, COLS // 16, build, 0, unroll=4)

    arrived(0, 1, 3, 5, 6)
    mode = lax.broadcasted_iota(jnp.int32, (128, 128), 0)

    def digit(x, unit):
        return sum((x >= unit * k).astype(jnp.int32) for k in range(1, 5))

    first = digit(mode, 25)
    second = digit(mode - 25 * first, 5)
    third = mode - 25 * first - 5 * second
    highest = jnp.maximum(jnp.maximum(first, second), third)
    highest = jnp.where(mode < 125, highest, 99)
    for lt in range(2):
        lanes = slice(lt * 128, (lt + 1) * 128)
        act = (highest <= degrees[...].reshape(1, E)[:, lanes]).astype(F32)
        active[:, lanes] = act
        for b in range(NV):
            us[0, b, 125:128, lanes] = jnp.zeros((3, 128), F32)
            us[0, b, 0:125, lanes] = src[b, :, lanes] * act[0:125]
    jac2[...] = jac[...] * 0.2

    r24 = lax.broadcasted_iota(jnp.int32, (24, ROWS), 0)
    c24 = lax.broadcasted_iota(jnp.int32, (24, ROWS), 1)
    r16 = lax.broadcasted_iota(jnp.int32, (16, ROWS), 0)
    c16 = lax.broadcasted_iota(jnp.int32, (16, ROWS), 1)
    mixed = []
    for mat in (diss, conv):
        parts = []
        for x in range(NV):
            acc = jnp.zeros((24, ROWS), F32)
            for y in range(NV):
                acc = acc + jnp.where(c24 == r24 + y * 24, mat[x, y], 0.0)
            parts.append(acc)
        acc = jnp.zeros((16, ROWS), F32)
        for x in range(NV):
            for y in range(NV):
                acc = acc + jnp.where((r16 == x) & (c16 == 144 + y), mat[x, y], 0.0)
        parts.append(acc)
        mixed.append(jnp.concatenate(parts, axis=0))
    mixed = jnp.concatenate(mixed, axis=1)
    mix_hi, mix_lo = split(mixed)
    mix[:, 0 : 2 * ROWS] = mix_hi
    mix[:, 2 * ROWS : 4 * ROWS] = mix_hi
    mix[:, 4 * ROWS : 6 * ROWS] = mix_lo

    flat[...] = jnp.zeros_like(flat)
    faces[...] = jnp.zeros_like(faces)
    for s in range(4):

        @pl.when(jnp.logical_not(has[s]))
        def _(s=s):
            for k in range(ITERS):
                recvs[k, s] = jnp.zeros((SEND, FS), F32)

    arrived(2, 4, 7, 12, 13)
    mode_mat[:, 0:128] = mode_in[...].astype(BF)
    mode_mat[:, 128:256] = mode_in[...].astype(BF)
    lift_mat[...] = lift_in[...].astype(BF)
    pl.semaphore_wait(barrier, n_span + n_chord - 2)

    def side_copy(step, s):
        return pltpu.make_async_remote_copy(
            src_ref=sends.at[step, s],
            dst_ref=recvs.at[step, s ^ 1],
            send_sem=send_sem.at[step, s],
            recv_sem=recv_sem.at[step, s ^ 1],
            device_id=targets[s],
            device_id_type=MESH,
        )

    def mix_terms(difference, total):
        d_hi, d_lo = split(difference)
        t_hi, t_lo = split(total)
        n = difference.shape[1]
        for k, part in enumerate((d_hi, t_hi, d_lo, t_lo, d_hi, t_hi)):
            uv_b[k * ROWS : (k + 1) * ROWS, 0:n] = part
        return dot(mix[...], uv_b[:, 0:n])

    def one_step(step, carry):
        for lt in range(2):
            lanes = slice(lt * 128, (lt + 1) * 128)
            for a0 in range(0, NV, 2):
                acc = [None, None]
                for b in range(NV):
                    u = us[step, b, :, lanes]
                    for p in range(2):
                        t = binv[a0 + p, b : b + 1, lanes] * u
                        acc[p] = t if acc[p] is None else acc[p] + t
                for p in range(2):
                    zs[step, a0 + p, :, lanes] = acc[p]
                    hi, lo = split(acc[p])
                    modes[a0 + p, 0:128, lanes] = hi
                    modes[a0 + p, 128:256, lanes] = lo
        for b in range(NV):
            t = dot(mode_mat[0:ROWS, :], modes[b])
            for f in range(NF):
                flat[b * 24 : (b + 1) * 24, f * E : (f + 1) * E] = t[f * 24 : (f + 1) * 24]
                flat[144 + b : 145 + b, f * E : (f + 1) * E] = t[144 + f : 145 + f]
        for f in range(NF):
            hi, lo = split(flat[:, f * E : (f + 1) * E])
            flat_b[0:ROWS, f * E : (f + 1) * E] = hi
            flat_b[ROWS : 2 * ROWS, f * E : (f + 1) * E] = lo
        t = dot(flat_b[...], select[:, 2 * IF :])
        own[...] = t[0:ROWS] + t[ROWS:]
        for s in range(4):
            sends[step, s] = own[0:SEND, s * FS : (s + 1) * FS]

            @pl.when(has[s])
            def _(s=s):
                side_copy(step, s).start()

        for b in range(NV):
            grads[b] = dot(mode_mat[ROWS:, :], modes[b])
        for q in range(2):
            t = dot(flat_b[...], select[:, q * IF : (q + 1) * IF])
            interior[q] = t[0:ROWS] + t[ROWS:]
        term = mix_terms(interior[0], interior[1]) * weight[...].reshape(1, IF)
        hi, lo = split(term)
        term_b[0:ROWS] = hi
        term_b[ROWS:] = lo
        for f in range(NF):
            t = dot_t(term_b[...], select[f * E : (f + 1) * E, 0:IF])
            gathered[:, f * E : (f + 1) * E] = t[0:ROWS] + t[ROWS:]
        for lt in range(2):
            lanes = slice(lt * 128, (lt + 1) * 128)
            shift = time_shift[...].reshape(1, E)[:, lanes]
            for a0 in range(0, NV, 2):
                acc = [shift * zs[step, a0 + p, :, lanes] for p in range(2)]
                for d in range(3):
                    for b in range(NV):
                        g = grads[b, d * 128 : (d + 1) * 128, lanes]
                        for p in range(2):
                            acc[p] = acc[p] + jac2[d, a0 + p, b : b + 1, lanes] * g
                for p in range(2):
                    us[step + 1, a0 + p, :, lanes] = acc[p]
        for s in range(4):

            @pl.when(has[s])
            def _(s=s):
                side_copy(step, s ^ 1).wait_recv()

        diffs, sums = [], []
        for s in range(4):
            mine = own[:, s * FS : (s + 1) * FS]
            other = jnp.concatenate([recvs[step, s], jnp.zeros((ROWS - SEND, FS), F32)], axis=0)
            diffs.append(mine - other)
            sums.append(mine + other if s % 2 == 1 else -(mine + other))
        term = mix_terms(jnp.concatenate(diffs, axis=1), jnp.concatenate(sums, axis=1))
        hi, lo = split(term)
        term_b[0:ROWS] = hi
        term_b[ROWS:] = lo
        for f in range(NF):
            t = dot_t(term_b[...], select[f * E : (f + 1) * E, 2 * IF :])
            t = gathered[:, f * E : (f + 1) * E] + (t[0:ROWS] + t[ROWS:])
            for b in range(NV):
                faces[b, f * 24 : (f + 1) * 24, :] = t[b * 24 : (b + 1) * 24]
                faces[b, 144 + f : 145 + f, :] = t[144 + b : 145 + b]
        for b in range(NV):
            hi, lo = split(faces[b])
            t = dot(lift_mat[...], jnp.concatenate([hi, lo], axis=0))
            us[step + 1, b] = (us[step + 1, b] + t) * active[...] - SHIFT * us[step, b]
        for s in range(4):

            @pl.when(has[s])
            def _(s=s):
                side_copy(step, s).wait_send()

        return carry

    lax.fori_loop(0, ITERS, one_step, 0)

    pairs = [(i, j) for i in range(ITERS + 1) for j in range(i, ITERS + 1)]

    def products(c, accs):
        accs = list(accs)
        base = pl.multiple_of(c * 8, 8)
        for b in range(NV):
            for lt in range(2):
                lanes = slice(lt * 128, (lt + 1) * 128)
                u = [us[k, b, pl.ds(base, 8), lanes] for k in range(ITERS + 1)]
                for n, (i, j) in enumerate(pairs):
                    accs[n] = accs[n] + u[i] * u[j]
        return tuple(accs)

    accs = lax.fori_loop(0, 16, products, tuple(jnp.zeros((8, 128), F32) for _ in pairs))
    rows = [jnp.sum(x, axis=0, keepdims=True) for x in accs]
    rows.append(jnp.zeros((1, 128), F32))
    x = jnp.concatenate(rows, axis=0)
    for amount in (64, 32, 16, 8):
        x = x + pltpu.roll(x, amount, 1)
    row = lax.broadcasted_iota(jnp.int32, (16, 128), 0)
    lane = lax.broadcasted_iota(jnp.int32, (16, 128), 1)
    x = jnp.sum(jnp.where((lane >= row * 8) & (lane < row * 8 + 8), x, 0.0), axis=0, keepdims=True)
    gram[0] = jnp.broadcast_to(x, (8, 128))

    def r1_copy(i):
        return pltpu.make_async_remote_copy(
            src_ref=gram.at[0],
            dst_ref=red1.at[i],
            send_sem=r1_send.at[i],
            recv_sem=r1_recv.at[i],
            device_id=(lax.rem(span + i, n_span), chord),
            device_id_type=MESH,
        )

    def r2_copy(i):
        return pltpu.make_async_remote_copy(
            src_ref=gram.at[1],
            dst_ref=red2.at[i],
            send_sem=r2_send.at[i],
            recv_sem=r2_recv.at[i],
            device_id=(span, lax.rem(chord + i, n_chord)),
            device_id_type=MESH,
        )

    for i in range(1, n_span):
        r1_copy(i).start()
    total = gram[0]
    for i in range(1, n_span):
        r1_copy(i).wait_recv()
        total = total + red1[i]
    gram[1] = total
    for i in range(1, n_chord):
        r2_copy(i).start()
    total = gram[1]
    for i in range(1, n_chord):
        r2_copy(i).wait_recv()
        total = total + red2[i]
    for amount in (4, 2, 1):
        total = total + pltpu.roll(total, 128 - amount, 1)

    g = {}
    for n, (i, j) in enumerate(pairs):
        g[i, j] = g[j, i] = jnp.broadcast_to(total[:, 8 * n : 8 * n + 1], (8, 128))
    half = [[SHIFT * g[i, j] + g[i, j + 1] for j in range(ITERS)] for i in range(ITERS + 1)]
    normal = [
        [SHIFT * half[i][j] + half[i + 1][j] for j in range(ITERS)] for i in range(ITERS)
    ]
    rhs = [half[0][j] for j in range(ITERS)]
    low = [[None] * ITERS for _ in range(ITERS)]
    pivot, inv = [], []
    for j in range(ITERS):
        d = normal[j][j]
        for k in range(j):
            d = d - low[j][k] * low[j][k] * pivot[k]
        pivot.append(d)
        usable = d > 1e-6 * normal[j][j]
        inv.append(jnp.where(usable, 1.0 / jnp.where(usable, d, 1.0), 0.0))
        for i in range(j + 1, ITERS):
            v = normal[i][j]
            for k in range(j):
                v = v - low[i][k] * low[j][k] * pivot[k]
            low[i][j] = v * inv[j]
    y = []
    for i in range(ITERS):
        v = rhs[i]
        for k in range(i):
            v = v - low[i][k] * y[k]
        y.append(v)
    coeffs = [y[i] * inv[i] for i in range(ITERS)]
    for i in reversed(range(ITERS)):
        for k in range(i + 1, ITERS):
            coeffs[i] = coeffs[i] - low[k][i] * coeffs[k]
    coeffs = [c[0:1, :] for c in coeffs]
    for b in range(NV):
        for lt in range(2):
            lanes = slice(lt * 128, (lt + 1) * 128)
            x = coeffs[0] * zs[0, b, 0:125, lanes]
            for k in range(1, ITERS):
                x = x + coeffs[k] * zs[k, b, 0:125, lanes]
            out[b, :, lanes] = x

    for i in range(1, n_span):
        r1_copy(i).wait_send()
    for i in range(1, n_chord):
        r2_copy(i).wait_send()


def local(n_span, n_chord, *args):
    args = args + constants()
    held = [(pltpu.SMEM if k in (5, 6) else pltpu.VMEM)(a.shape, a.dtype) for k, a in enumerate(args)]
    return pl.pallas_call(
        functools.partial(kernel, n_span, n_chord),
        out_shape=jax.ShapeDtypeStruct((NV, 125, E), F32),
        in_specs=[pl.BlockSpec(memory_space=pltpu.HBM)] * len(args),
        out_specs=pl.BlockSpec(memory_space=pltpu.VMEM),
        scratch_shapes=held
        + [
            pltpu.SemaphoreType.DMA((len(args),)),
            pltpu.VMEM((ROWS + 384, 256), BF),
            pltpu.VMEM((128, 2 * ROWS), BF),
            pltpu.VMEM((128, E), F32),
            pltpu.VMEM((3, NV, NV, E), F32),
            pltpu.VMEM((COLS, SLOTS), BF),
            pltpu.VMEM((ROWS, 6 * ROWS), BF),
            pltpu.VMEM((ITERS + 1, NV, 128, E), F32),
            pltpu.VMEM((ITERS, NV, 128, E), F32),
            pltpu.VMEM((NV, 256, E), BF),
            pltpu.VMEM((NV, 384, E), F32),
            pltpu.VMEM((ROWS, COLS), F32),
            pltpu.VMEM((2 * ROWS, COLS), BF),
            pltpu.VMEM((ROWS, 4 * FS), F32),
            pltpu.VMEM((2, ROWS, IF), F32),
            pltpu.VMEM((6 * ROWS, IF), BF),
            pltpu.VMEM((2 * ROWS, IF), BF),
            pltpu.VMEM((ROWS, COLS), F32),
            pltpu.VMEM((NV, ROWS, E), F32),
            pltpu.VMEM((ITERS, 4, SEND, FS), F32),
            pltpu.VMEM((ITERS, 4, SEND, FS), F32),
            pltpu.VMEM((2, 8, 128), F32),
            pltpu.VMEM((n_span, 8, 128), F32),
            pltpu.VMEM((n_chord, 8, 128), F32),
            pltpu.SemaphoreType.DMA((ITERS, 4)),
            pltpu.SemaphoreType.DMA((ITERS, 4)),
            pltpu.SemaphoreType.DMA((n_span,)),
            pltpu.SemaphoreType.DMA((n_span,)),
            pltpu.SemaphoreType.DMA((n_chord,)),
            pltpu.SemaphoreType.DMA((n_chord,)),
        ],
        compiler_params=pltpu.CompilerParams(
            collective_id=0, has_side_effects=True, vmem_limit_bytes=60 * 1024 * 1024
        ),
    )(*args)


def solution(mesh):
    placed = (
        P(None, None, ("span", "chord")),
        P(("span", "chord")),
        P(("span", "chord")),
        P(None, None, None, ("span", "chord")),
        P(None, None, ("span", "chord")),
        P(),
        P(),
        P(("span", "chord")),
        P(None, ("span", "chord")),
        P(None, ("span", "chord")),
        P(None, ("span", "chord")),
        P(None, ("span", "chord")),
    )
    return jax.shard_map(
        functools.partial(local, mesh.shape["span"], mesh.shape["chord"]),
        mesh=mesh,
        in_specs=placed,
        out_specs=P(None, None, ("span", "chord")),
        check_vma=False,
    )
```

```python
import functools

import jax
import jax.numpy as jnp
import numpy as np
from jax import lax
from jax.experimental import pallas as pl
from jax.experimental.pallas import tpu as pltpu
from jax.sharding import PartitionSpec as P

ITERS = 4
NV = 6
E = 256
IF = 512
FS = 128
NF = 6
ROWS = 160
SEND = 152
COLS = NF * E
SLOTS = 2 * IF + 4 * FS
SHIFT = 1.5
FULL_STEPS = 2
LOAD_ORDER = (8, 9, 10, 11, 0, 1, 4, 12, 3, 5, 6, 7, 2, 13)
STAGES = (("span", 1, 8), ("chord", 1, 16))
MESH = pl.DeviceIdType.MESH
BF = jnp.bfloat16
F32 = jnp.float32


def face_row(face, t):
    return face * 24 + t if t < 24 else 144 + face


def constants():
    mode_mat = np.zeros((ROWS + 384, 128), np.float32)
    lift = np.zeros((128, ROWS), np.float32)
    sign = [1.0, -1.0, 1.0, -1.0, 1.0]
    for i in range(5):
        for j in range(5):
            for k in range(5):
                m = 25 * i + 5 * j + k
                idx = (i, j, k)
                rest = (5 * j + k, 5 * i + k, 5 * i + j)
                step = (25, 5, 1)
                for d in range(3):
                    for end in range(2):
                        r = face_row(2 * d + end, rest[d])
                        value = 0.5 * (sign[idx[d]] if end == 0 else 1.0)
                        mode_mat[r, m] = value
                        lift[m, r] = value
                    for low in range(idx[d]):
                        if (idx[d] - low) % 2 == 1:
                            out = m - step[d] * (idx[d] - low)
                            mode_mat[ROWS + 128 * d + out, m] = 2 * low + 1
    return (
        jnp.asarray(mode_mat),
        jnp.asarray(np.concatenate([lift, lift], axis=1)),
    )


def split(x):
    hi = x.astype(BF)
    return hi, (x - hi.astype(F32)).astype(BF)


def dot(a, b):
    return jnp.dot(a, b, preferred_element_type=F32)


def dot_t(a, b):
    return lax.dot_general(a, b, (((1,), (1,)), ((), ())), preferred_element_type=F32)


def kernel(
    n_span,
    n_chord,
    *refs,
):
    operands, out, refs = refs[:14], refs[14], refs[15:]
    held, load_sem, refs = refs[:14], refs[14], refs[15:]
    (
        src,
        degrees,
        time_shift,
        jac,
        binv,
        diss,
        conv,
        weight,
        face_el,
        face_no,
        side_el,
        side_no,
        mode_in,
        lift_in,
    ) = held
    (
        mode_mat,
        lift_mat,
        active,
        jac2,
        select,
        mix,
        us,
        zs,
        modes,
        grads,
        flat,
        flat_b,
        own,
        uv_b,
        term_b,
        gathered,
        faces,
        sends,
        recvs,
        gram,
        sums_in,
        send_sem,
        recv_sem,
        sum_send,
        sum_recv,
    ) = refs
    loads = [pltpu.make_async_copy(a, b, load_sem.at[k]) for k, (a, b) in enumerate(zip(operands, held))]
    for k in LOAD_ORDER:
        loads[k].start()

    def arrived(*which):
        for k in which:
            loads[k].wait()

    span = lax.axis_index("span")
    chord = lax.axis_index("chord")

    barrier = pltpu.get_barrier_semaphore()
    def partner(stage, i):
        axis, stride, size = STAGES[stage]
        index = span if axis == "span" else chord
        digit = lax.rem(index // stride, size)
        index = index + (lax.rem(digit + i, size) - digit) * stride
        return (index, chord) if axis == "span" else (span, index)

    partners = [(k, i) for k, stage in enumerate(STAGES) for i in range(1, stage[2])]
    for k, i in partners:
        pl.semaphore_signal(barrier, inc=1, device_id=partner(k, i), device_id_type=MESH)

    has = (span > 0, span < n_span - 1, chord > 0, chord < n_chord - 1)
    has = [h.astype(F32) for h in has]
    targets = (
        (lax.rem(span + n_span - 1, n_span), chord),
        (lax.rem(span + 1, n_span), chord),
        (span, lax.rem(chord + n_chord - 1, n_chord)),
        (span, lax.rem(chord + 1, n_chord)),
    )

    arrived(8, 9, 10, 11)
    cols_in = face_no[...] * E + face_el[...]
    cols_sd = side_no[...] * E + side_el[...]
    left = cols_in[0:1, :]
    right = cols_in[1:2, :]
    row16 = lax.broadcasted_iota(jnp.int32, (16, FS), 0)

    def build(c, carry):
        base = pl.multiple_of(c * 16, 16)
        rows = row16 + base
        for q in range(4):
            l = (rows == left[:, q * FS : (q + 1) * FS]).astype(F32)
            r = (rows == right[:, q * FS : (q + 1) * FS]).astype(F32)
            s = (rows == cols_sd[q : q + 1, :]).astype(F32)
            select[pl.ds(base, 16), IF + q * FS : IF + (q + 1) * FS] = (l - r).astype(BF)
            select[pl.ds(base, 16), q * FS : (q + 1) * FS] = (l + r).astype(BF)
            select[pl.ds(base, 16), 2 * IF + q * FS : 2 * IF + (q + 1) * FS] = s.astype(BF)
        return carry

    lax.fori_loop(0, COLS // 16, build, 0, unroll=4)

    arrived(0, 1, 3, 5, 6)
    mode = lax.broadcasted_iota(jnp.int32, (128, 128), 0)

    def digit(x, unit):
        return sum((x >= unit * k).astype(jnp.int32) for k in range(1, 5))

    first = digit(mode, 25)
    second = digit(mode - 25 * first, 5)
    third = mode - 25 * first - 5 * second
    highest = jnp.maximum(jnp.maximum(first, second), third)
    highest = jnp.where(mode < 125, highest, 99)
    for lt in range(2):
        lanes = slice(lt * 128, (lt + 1) * 128)
        act = (highest <= degrees[...].reshape(1, E)[:, lanes]).astype(F32)
        active[:, lanes] = act
        for b in range(NV):
            us[0, b, 125:128, lanes] = jnp.zeros((3, 128), F32)
            us[0, b, 0:125, lanes] = src[b, :, lanes] * act[0:125]
    jac2[...] = jac[...] * 0.2

    r24 = lax.broadcasted_iota(jnp.int32, (24, ROWS), 0)
    c24 = lax.broadcasted_iota(jnp.int32, (24, ROWS), 1)
    r16 = lax.broadcasted_iota(jnp.int32, (16, ROWS), 0)
    c16 = lax.broadcasted_iota(jnp.int32, (16, ROWS), 1)
    mixed = []
    for mat in (diss, conv):
        parts = []
        for x in range(NV):
            acc = jnp.zeros((24, ROWS), F32)
            for y in range(NV):
                acc = acc + jnp.where(c24 == r24 + y * 24, mat[x, y], 0.0)
            parts.append(acc)
        acc = jnp.zeros((16, ROWS), F32)
        for x in range(NV):
            for y in range(NV):
                acc = acc + jnp.where((r16 == x) & (c16 == 144 + y), mat[x, y], 0.0)
        parts.append(acc)
        mixed.append(jnp.concatenate(parts, axis=0))
    mixed = jnp.concatenate(mixed, axis=1)
    mix_hi, mix_lo = split(mixed)
    mix[:, 0 : 2 * ROWS] = mix_hi
    mix[:, 2 * ROWS : 4 * ROWS] = mix_hi
    mix[:, 4 * ROWS : 6 * ROWS] = mix_lo

    flat[...] = jnp.zeros_like(flat)
    faces[...] = jnp.zeros_like(faces)
    arrived(2, 4, 7, 12, 13)
    mode_mat[:, 0:128] = mode_in[...].astype(BF)
    mode_mat[:, 128:256] = mode_in[...].astype(BF)
    lift_mat[...] = lift_in[...].astype(BF)
    pl.semaphore_wait(barrier, len(partners))

    def side_copy(step, s):
        return pltpu.make_async_remote_copy(
            src_ref=sends.at[step, s],
            dst_ref=recvs.at[step, s ^ 1],
            send_sem=send_sem.at[step, s],
            recv_sem=recv_sem.at[step, s ^ 1],
            device_id=targets[s],
            device_id_type=MESH,
        )

    def mix_terms(difference, total, full):
        n = difference.shape[1]
        d_hi, d_lo = split(difference)
        t_hi, t_lo = split(total)
        parts = (d_hi, t_hi, d_lo, t_lo, d_hi, t_hi) if full else (d_hi, t_hi)
        for k, part in enumerate(parts):
            uv_b[k * ROWS : (k + 1) * ROWS, 0:n] = part
        return dot(mix[:, 0 : len(parts) * ROWS], uv_b[0 : len(parts) * ROWS, 0:n])

    def store_parts(ref, x, row, cols, full):
        hi, lo = split(x)
        n = x.shape[0]
        ref[row : row + n, cols] = hi
        if full:
            ref[ROWS + row : ROWS + row + n, cols] = lo

    def both(t, full):
        return t[0:ROWS] + t[ROWS:] if full else t

    def one_step(full, step, carry):
        used = 2 * ROWS if full else ROWS
        for a0 in range(0, NV, 2):
            for lt in range(2):
                lanes = slice(lt * 128, (lt + 1) * 128)
                acc = [None, None]
                for b in range(NV):
                    u = us[step, b, :, lanes]
                    for p in range(2):
                        t = binv[a0 + p, b : b + 1, lanes] * u
                        acc[p] = t if acc[p] is None else acc[p] + t
                for p in range(2):
                    zs[step, a0 + p, :, lanes] = acc[p]
                    hi, lo = split(acc[p])
                    modes[a0 + p, 0:128, lanes] = hi
                    modes[a0 + p, 128:256, lanes] = lo
            for b in (a0, a0 + 1):
                t = dot(mode_mat[0:ROWS, :], modes[b])
                for f in range(NF):
                    cols = slice(f * E, (f + 1) * E)
                    flat[b * 24 : (b + 1) * 24, cols] = t[f * 24 : (f + 1) * 24]
                    flat[144 + b : 145 + b, cols] = t[144 + f : 145 + f]
            store_parts(flat_b, flat[a0 * 24 : (a0 + 2) * 24, :], a0 * 24, slice(0, COLS), full)
        store_parts(flat_b, flat[144:ROWS, :], 144, slice(0, COLS), full)
        for pair in (1, 0):
            cols = slice(2 * IF + pair * 2 * FS, 2 * IF + (pair + 1) * 2 * FS)
            t = both(dot(flat_b[0:used], select[:, cols]), full)
            own[:, pair * 2 * FS : (pair + 1) * 2 * FS] = t
            for s in (2 * pair, 2 * pair + 1):
                sends[step, s] = t[0:SEND, (s % 2) * FS : (s % 2 + 1) * FS]
                side_copy(step, s).start()

        for b in range(NV):
            grads[b] = dot(mode_mat[ROWS:, :], modes[b])
        def volume(a0, lt):
            lanes = slice(lt * 128, (lt + 1) * 128)
            shift = time_shift[...].reshape(1, E)[:, lanes]
            acc = [shift * zs[step, a0 + p, :, lanes] for p in range(2)]
            for d in range(3):
                for b in range(NV):
                    g = grads[b, d * 128 : (d + 1) * 128, lanes]
                    for p in range(2):
                        acc[p] = acc[p] + jac2[d, a0 + p, b : b + 1, lanes] * g
            for p in range(2):
                us[step + 1, a0 + p, :, lanes] = acc[p]

        volumes = [functools.partial(volume, a0, lt) for lt in range(2) for a0 in range(0, NV, 2)]

        for q in range(2):
            cols = slice(q * E, (q + 1) * E)
            total = both(dot(flat_b[0:used], select[:, cols]), full)
            volumes.pop()()
            difference = both(dot(flat_b[0:used], select[:, IF + q * E : IF + (q + 1) * E]), full)
            volumes.pop()()
            term = mix_terms(difference, total, full) * weight[...].reshape(1, IF)[:, cols]
            store_parts(term_b, term, 0, cols, full)
            volumes.pop()()

        def side_terms(pair):
            diffs, totals = [], []
            for s in (2 * pair, 2 * pair + 1):
                side_copy(step, s ^ 1).wait_recv()
                mine = own[:, s * FS : (s + 1) * FS]
                other = recvs[step, s] * has[s]
                other = jnp.concatenate([other, jnp.zeros((ROWS - SEND, FS), F32)], axis=0)
                diffs.append(mine - other)
                totals.append(mine + other if s % 2 == 1 else -(mine + other))
            term = mix_terms(jnp.concatenate(diffs, axis=1), jnp.concatenate(totals, axis=1), full)
            start = IF + pair * 2 * FS
            store_parts(term_b, term, 0, slice(start, start + 2 * FS), full)

        def scattered(f, start, stop):
            return both(
                dot_t(term_b[0:used, start:stop], select[f * E : (f + 1) * E, IF + start : IF + stop]),
                full,
            )

        side_terms(0)
        for f in range(NF):
            gathered[:, f * E : (f + 1) * E] = scattered(f, 0, IF + 2 * FS)
        side_terms(1)
        for f in range(NF):
            t = gathered[:, f * E : (f + 1) * E] + scattered(f, IF + 2 * FS, IF + 4 * FS)
            for b in range(NV):
                faces[b, f * 24 : (f + 1) * 24, :] = t[b * 24 : (b + 1) * 24]
                faces[b, 144 + f : 145 + f, :] = t[144 + b : 145 + b]
        for b in range(NV):
            hi, lo = split(faces[b])
            if full:
                t = dot(lift_mat[...], jnp.concatenate([hi, lo], axis=0))
            else:
                t = dot(lift_mat[:, 0:ROWS], hi)
            us[step + 1, b] = (us[step + 1, b] + t) * active[...] - SHIFT * us[step, b]
        for s in range(4):
            side_copy(step, s).wait_send()
        return carry

    lax.fori_loop(0, FULL_STEPS, functools.partial(one_step, True), 0)
    lax.fori_loop(FULL_STEPS, ITERS, functools.partial(one_step, False), 0)

    pairs = [(i, j) for i in range(ITERS + 1) for j in range(i, ITERS + 1)]

    def products(c, accs):
        accs = list(accs)
        base = pl.multiple_of(c * 8, 8)
        for b in range(NV):
            for lt in range(2):
                lanes = slice(lt * 128, (lt + 1) * 128)
                u = [us[k, b, pl.ds(base, 8), lanes] for k in range(ITERS + 1)]
                for n, (i, j) in enumerate(pairs):
                    accs[n] = accs[n] + u[i] * u[j]
        return tuple(accs)

    accs = lax.fori_loop(0, 16, products, tuple(jnp.zeros((8, 128), F32) for _ in pairs))
    rows = [jnp.sum(x, axis=0, keepdims=True) for x in accs]
    rows.append(jnp.zeros((1, 128), F32))
    x = jnp.concatenate(rows, axis=0)
    for amount in (64, 32, 16, 8):
        x = x + pltpu.roll(x, amount, 1)
    row = lax.broadcasted_iota(jnp.int32, (16, 128), 0)
    lane = lax.broadcasted_iota(jnp.int32, (16, 128), 1)
    x = jnp.sum(jnp.where((lane >= row * 8) & (lane < row * 8 + 8), x, 0.0), axis=0, keepdims=True)
    gram[0] = jnp.broadcast_to(x, (8, 128))

    def sum_copy(k, i):
        return pltpu.make_async_remote_copy(
            src_ref=gram.at[k],
            dst_ref=sums_in.at[k, i],
            send_sem=sum_send.at[k, i],
            recv_sem=sum_recv.at[k, i],
            device_id=partner(k, i),
            device_id_type=MESH,
        )

    total = gram[0]
    for k, (_, _, size) in enumerate(STAGES):
        if k > 0:
            gram[k] = total
        for i in range(1, size):
            sum_copy(k, i).start()
        for i in range(1, size):
            sum_copy(k, i).wait_recv()
            total = total + sums_in[k, i]
    for amount in (4, 2, 1):
        total = total + pltpu.roll(total, 128 - amount, 1)

    g = {}
    for n, (i, j) in enumerate(pairs):
        g[i, j] = g[j, i] = jnp.broadcast_to(total[:, 8 * n : 8 * n + 1], (8, 128))
    half = [[SHIFT * g[i, j] + g[i, j + 1] for j in range(ITERS)] for i in range(ITERS + 1)]
    normal = [
        [SHIFT * half[i][j] + half[i + 1][j] for j in range(ITERS)] for i in range(ITERS)
    ]
    rhs = [half[0][j] for j in range(ITERS)]
    low = [[None] * ITERS for _ in range(ITERS)]
    pivot, inv = [], []
    for j in range(ITERS):
        d = normal[j][j]
        for k in range(j):
            d = d - low[j][k] * low[j][k] * pivot[k]
        pivot.append(d)
        usable = d > 1e-6 * normal[j][j]
        inv.append(jnp.where(usable, 1.0 / jnp.where(usable, d, 1.0), 0.0))
        for i in range(j + 1, ITERS):
            v = normal[i][j]
            for k in range(j):
                v = v - low[i][k] * low[j][k] * pivot[k]
            low[i][j] = v * inv[j]
    y = []
    for i in range(ITERS):
        v = rhs[i]
        for k in range(i):
            v = v - low[i][k] * y[k]
        y.append(v)
    coeffs = [y[i] * inv[i] for i in range(ITERS)]
    for i in reversed(range(ITERS)):
        for k in range(i + 1, ITERS):
            coeffs[i] = coeffs[i] - low[k][i] * coeffs[k]
    for b in range(NV):
        for lt in range(2):
            lanes = slice(lt * 128, (lt + 1) * 128)
            x = coeffs[0][0:1] * zs[0, b, 0:125, lanes]
            for k in range(1, ITERS):
                x = x + coeffs[k][0:1] * zs[k, b, 0:125, lanes]
            out[b, :, lanes] = x
    for k, i in partners:
        sum_copy(k, i).wait_send()


def local(n_span, n_chord, *args):
    args = tuple(pltpu.with_memory_space_constraint(a, pltpu.HBM) for a in args + constants())
    held = [(pltpu.SMEM if k in (5, 6) else pltpu.VMEM)(a.shape, a.dtype) for k, a in enumerate(args)]
    return pl.pallas_call(
        functools.partial(kernel, n_span, n_chord),
        out_shape=jax.ShapeDtypeStruct((NV, 125, E), F32),
        in_specs=[pl.BlockSpec(memory_space=pltpu.HBM)] * len(args),
        out_specs=pl.BlockSpec(memory_space=pltpu.VMEM),
        scratch_shapes=held
        + [
            pltpu.SemaphoreType.DMA((len(args),)),
            pltpu.VMEM((ROWS + 384, 256), BF),
            pltpu.VMEM((128, 2 * ROWS), BF),
            pltpu.VMEM((128, E), F32),
            pltpu.VMEM((3, NV, NV, E), F32),
            pltpu.VMEM((COLS, SLOTS), BF),
            pltpu.VMEM((ROWS, 6 * ROWS), BF),
            pltpu.VMEM((ITERS + 1, NV, 128, E), F32),
            pltpu.VMEM((ITERS, NV, 128, E), F32),
            pltpu.VMEM((NV, 256, E), BF),
            pltpu.VMEM((NV, 384, E), F32),
            pltpu.VMEM((ROWS, COLS), F32),
            pltpu.VMEM((2 * ROWS, COLS), BF),
            pltpu.VMEM((ROWS, 4 * FS), F32),
            pltpu.VMEM((6 * ROWS, IF), BF),
            pltpu.VMEM((2 * ROWS, IF + 4 * FS), BF),
            pltpu.VMEM((ROWS, COLS), F32),
            pltpu.VMEM((NV, ROWS, E), F32),
            pltpu.VMEM((ITERS, 4, SEND, FS), F32),
            pltpu.VMEM((ITERS, 4, SEND, FS), F32),
            pltpu.VMEM((len(STAGES), 8, 128), F32),
            pltpu.VMEM((len(STAGES), 16, 8, 128), F32),
            pltpu.SemaphoreType.DMA((ITERS, 4)),
            pltpu.SemaphoreType.DMA((ITERS, 4)),
            pltpu.SemaphoreType.DMA((len(STAGES), 16)),
            pltpu.SemaphoreType.DMA((len(STAGES), 16)),
        ],
        compiler_params=pltpu.CompilerParams(
            collective_id=0, has_side_effects=True, vmem_limit_bytes=44 * 1024 * 1024
        ),
    )(*args)


def solution(mesh):
    placed = (
        P(None, None, ("span", "chord")),
        P(("span", "chord")),
        P(("span", "chord")),
        P(None, None, None, ("span", "chord")),
        P(None, None, ("span", "chord")),
        P(),
        P(),
        P(("span", "chord")),
        P(None, ("span", "chord")),
        P(None, ("span", "chord")),
        P(None, ("span", "chord")),
        P(None, ("span", "chord")),
    )
    return jax.shard_map(
        functools.partial(local, mesh.shape["span"], mesh.shape["chord"]),
        mesh=mesh,
        in_specs=placed,
        out_specs=P(None, None, ("span", "chord")),
        check_vma=False,
    )
```

```python
import functools

import jax
import jax.numpy as jnp
import numpy as np
from jax import lax
from jax.experimental import pallas as pl
from jax.experimental.pallas import tpu as pltpu
from jax.sharding import PartitionSpec as P

ITERS = 4
NV = 6
E = 256
IF = 512
FS = 128
NF = 6
ROWS = 160
SEND = 152
COLS = NF * E
SLOTS = 2 * IF + 4 * FS
SHIFT = 1.5
FULL_STEPS = 2
LOAD_ORDER = (8, 9, 10, 11, 0, 1, 4, 12, 3, 5, 6, 7, 2, 13)
STAGES = (("span", 1, 8), ("chord", 1, 16))
MESH = pl.DeviceIdType.MESH
BF = jnp.bfloat16
F32 = jnp.float32


def face_row(face, t):
    return face * 24 + t if t < 24 else 144 + face


def constants():
    mode_mat = np.zeros((ROWS + 384, 128), np.float32)
    lift = np.zeros((128, ROWS), np.float32)
    sign = [1.0, -1.0, 1.0, -1.0, 1.0]
    for i in range(5):
        for j in range(5):
            for k in range(5):
                m = 25 * i + 5 * j + k
                idx = (i, j, k)
                rest = (5 * j + k, 5 * i + k, 5 * i + j)
                step = (25, 5, 1)
                for d in range(3):
                    for end in range(2):
                        r = face_row(2 * d + end, rest[d])
                        value = 0.5 * (sign[idx[d]] if end == 0 else 1.0)
                        mode_mat[r, m] = value
                        lift[m, r] = value
                    for low in range(idx[d]):
                        if (idx[d] - low) % 2 == 1:
                            out = m - step[d] * (idx[d] - low)
                            mode_mat[ROWS + 128 * d + out, m] = 2 * low + 1
    return (
        jnp.asarray(mode_mat),
        jnp.asarray(np.concatenate([lift, lift], axis=1)),
    )


def split(x):
    hi = x.astype(BF)
    return hi, (x - hi.astype(F32)).astype(BF)


def dot(a, b):
    return jnp.dot(a, b, preferred_element_type=F32)


def dot_t(a, b):
    return lax.dot_general(a, b, (((1,), (1,)), ((), ())), preferred_element_type=F32)


def kernel(
    n_span,
    n_chord,
    *refs,
):
    operands, out, refs = refs[:14], refs[14], refs[15:]
    held, load_sem, refs = refs[:14], refs[14], refs[15:]
    (
        src,
        degrees,
        time_shift,
        jac,
        binv,
        diss,
        conv,
        weight,
        face_el,
        face_no,
        side_el,
        side_no,
        mode_in,
        lift_in,
    ) = held
    (
        mode_mat,
        lift_mat,
        active,
        jac2,
        select,
        mix,
        us,
        zs,
        modes,
        grads,
        flat,
        flat_b,
        uv_b,
        term_b,
        gathered,
        faces,
        sends,
        recvs,
        gram,
        sums_in,
        send_sem,
        recv_sem,
        sum_send,
        sum_recv,
        prods,
    ) = refs
    loads = [pltpu.make_async_copy(a, b, load_sem.at[k]) for k, (a, b) in enumerate(zip(operands, held))]
    for k in LOAD_ORDER:
        loads[k].start()

    def arrived(*which):
        for k in which:
            loads[k].wait()

    span = lax.axis_index("span")
    chord = lax.axis_index("chord")

    barrier = pltpu.get_barrier_semaphore()
    def partner(stage, i):
        axis, stride, size = STAGES[stage]
        index = span if axis == "span" else chord
        digit = lax.rem(index // stride, size)
        index = index + (lax.rem(digit + i, size) - digit) * stride
        return (index, chord) if axis == "span" else (span, index)

    partners = [(k, i) for k, stage in enumerate(STAGES) for i in range(1, stage[2])]
    for k, i in partners:
        pl.semaphore_signal(barrier, inc=1, device_id=partner(k, i), device_id_type=MESH)

    has = (span > 0, span < n_span - 1, chord > 0, chord < n_chord - 1)
    has = [h.astype(F32) for h in has]
    targets = (
        (lax.rem(span + n_span - 1, n_span), chord),
        (lax.rem(span + 1, n_span), chord),
        (span, lax.rem(chord + n_chord - 1, n_chord)),
        (span, lax.rem(chord + 1, n_chord)),
    )

    arrived(8, 9, 10, 11)
    cols_in = face_no[...] * E + face_el[...]
    cols_sd = side_no[...] * E + side_el[...]
    left = cols_in[0:1, :]
    right = cols_in[1:2, :]
    row16 = lax.broadcasted_iota(jnp.int32, (16, FS), 0)

    def build(c, carry):
        base = pl.multiple_of(c * 16, 16)
        rows = row16 + base
        for q in range(4):
            l = (rows == left[:, q * FS : (q + 1) * FS]).astype(F32)
            r = (rows == right[:, q * FS : (q + 1) * FS]).astype(F32)
            s = (rows == cols_sd[q : q + 1, :]).astype(F32)
            select[pl.ds(base, 16), IF + q * FS : IF + (q + 1) * FS] = (l - r).astype(BF)
            select[pl.ds(base, 16), q * FS : (q + 1) * FS] = (l + r).astype(BF)
            select[pl.ds(base, 16), 2 * IF + q * FS : 2 * IF + (q + 1) * FS] = s.astype(BF)
        return carry

    lax.fori_loop(0, COLS // 16, build, 0, unroll=4)

    arrived(0, 1, 3, 5, 6)
    mode = lax.broadcasted_iota(jnp.int32, (128, 128), 0)

    def digit(x, unit):
        return sum((x >= unit * k).astype(jnp.int32) for k in range(1, 5))

    first = digit(mode, 25)
    second = digit(mode - 25 * first, 5)
    third = mode - 25 * first - 5 * second
    highest = jnp.maximum(jnp.maximum(first, second), third)
    highest = jnp.where(mode < 125, highest, 99)
    for lt in range(2):
        lanes = slice(lt * 128, (lt + 1) * 128)
        act = (highest <= degrees[...].reshape(1, E)[:, lanes]).astype(F32)
        active[:, lanes] = act
        for b in range(NV):
            us[0, b, 125:128, lanes] = jnp.zeros((3, 128), F32)
            us[0, b, 0:125, lanes] = src[b, :, lanes] * act[0:125]
    jac2[...] = jac[...] * 0.2

    r24 = lax.broadcasted_iota(jnp.int32, (24, ROWS), 0)
    c24 = lax.broadcasted_iota(jnp.int32, (24, ROWS), 1)
    r16 = lax.broadcasted_iota(jnp.int32, (16, ROWS), 0)
    c16 = lax.broadcasted_iota(jnp.int32, (16, ROWS), 1)
    mixed = []
    for mat in (diss, conv):
        parts = []
        for x in range(NV):
            acc = jnp.zeros((24, ROWS), F32)
            for y in range(NV):
                acc = acc + jnp.where(c24 == r24 + y * 24, mat[x, y], 0.0)
            parts.append(acc)
        acc = jnp.zeros((16, ROWS), F32)
        for x in range(NV):
            for y in range(NV):
                acc = acc + jnp.where((r16 == x) & (c16 == 144 + y), mat[x, y], 0.0)
        parts.append(acc)
        mixed.append(jnp.concatenate(parts, axis=0))
    mixed = jnp.concatenate(mixed, axis=1)
    mix_hi, mix_lo = split(mixed)
    mix[:, 0 : 2 * ROWS] = mix_hi
    mix[:, 2 * ROWS : 4 * ROWS] = mix_hi
    mix[:, 4 * ROWS : 6 * ROWS] = mix_lo

    flat[...] = jnp.zeros_like(flat)
    faces[...] = jnp.zeros_like(faces)
    arrived(2, 4, 7, 12, 13)
    mode_mat[:, 0:128] = mode_in[...].astype(BF)
    mode_mat[:, 128:256] = mode_in[...].astype(BF)
    lift_mat[...] = lift_in[...].astype(BF)
    pl.semaphore_wait(barrier, len(partners))

    def side_copy(step, s):
        return pltpu.make_async_remote_copy(
            src_ref=sends.at[step, s],
            dst_ref=recvs.at[step, s ^ 1],
            send_sem=send_sem.at[step, s],
            recv_sem=recv_sem.at[step, s ^ 1],
            device_id=targets[s],
            device_id_type=MESH,
        )

    def mix_terms(difference, total, full):
        d_hi, d_lo = split(difference)
        t_hi, t_lo = split(total)
        parts = (d_hi, t_hi, d_lo, t_lo, d_hi, t_hi) if full else (d_hi, t_hi)
        for k, part in enumerate(parts):
            uv_b[k * ROWS : (k + 1) * ROWS, :] = part
        return dot(mix[:, 0 : len(parts) * ROWS], uv_b[0 : len(parts) * ROWS, :])

    def store_parts(ref, x, row, cols, full):
        hi, lo = split(x)
        n = x.shape[0]
        ref[row : row + n, cols] = hi
        if full:
            ref[ROWS + row : ROWS + row + n, cols] = lo

    def both(t, full):
        return t[0:ROWS] + t[ROWS:] if full else t

    early = [(i, j) for i in range(ITERS) for j in range(i, ITERS)]

    def early_products():
        def products(c, accs):
            accs = list(accs)
            base = pl.multiple_of(c * 8, 8)
            for b in range(NV):
                for lt in range(2):
                    lanes = slice(lt * 128, (lt + 1) * 128)
                    v = [us[k, b, pl.ds(base, 8), lanes] for k in range(ITERS)]
                    for n, (i, j) in enumerate(early):
                        accs[n] = accs[n] + v[i] * v[j]
            return tuple(accs)

        accs = lax.fori_loop(0, 16, products, (jnp.zeros((8, 128), F32),) * len(early))
        for n, acc in enumerate(accs):
            prods[n] = acc

    def one_step(full, step, carry):
        used = 2 * ROWS if full else ROWS
        for a0 in range(0, NV, 2):
            for lt in range(2):
                lanes = slice(lt * 128, (lt + 1) * 128)
                acc = [None, None]
                for b in range(NV):
                    u = us[step, b, :, lanes]
                    for p in range(2):
                        t = binv[a0 + p, b : b + 1, lanes] * u
                        acc[p] = t if acc[p] is None else acc[p] + t
                for p in range(2):
                    zs[step, a0 + p, :, lanes] = acc[p]
                    hi, lo = split(acc[p])
                    modes[a0 + p, 0:128, lanes] = hi
                    modes[a0 + p, 128:256, lanes] = lo
            for b in (a0, a0 + 1):
                t = dot(mode_mat[0:ROWS, :], modes[b])
                for f in range(NF):
                    cols = slice(f * E, (f + 1) * E)
                    flat[b * 24 : (b + 1) * 24, cols] = t[f * 24 : (f + 1) * 24]
                    flat[144 + b : 145 + b, cols] = t[144 + f : 145 + f]
            store_parts(flat_b, flat[a0 * 24 : (a0 + 2) * 24, :], a0 * 24, slice(0, COLS), full)
        store_parts(flat_b, flat[144:ROWS, :], 144, slice(0, COLS), full)
        for pair in (1, 0):
            cols = slice(2 * IF + pair * 2 * FS, 2 * IF + (pair + 1) * 2 * FS)
            t = both(dot(flat_b[0:used], select[:, cols]), full)
            for s in (2 * pair, 2 * pair + 1):
                sends[step, s] = t[0:SEND, (s % 2) * FS : (s % 2 + 1) * FS]
                side_copy(step, s).start()

        for b in range(NV):
            grads[b] = dot(mode_mat[ROWS:, :], modes[b])
        def volume(a0, lt):
            lanes = slice(lt * 128, (lt + 1) * 128)
            shift = time_shift[...].reshape(1, E)[:, lanes]
            acc = [shift * zs[step, a0 + p, :, lanes] for p in range(2)]
            for d in range(3):
                for b in range(NV):
                    g = grads[b, d * 128 : (d + 1) * 128, lanes]
                    for p in range(2):
                        acc[p] = acc[p] + jac2[d, a0 + p, b : b + 1, lanes] * g
            for p in range(2):
                us[step + 1, a0 + p, :, lanes] = acc[p]

        volumes = [functools.partial(volume, a0, lt) for lt in range(2) for a0 in range(0, NV, 2)]

        for q in range(2):
            cols = slice(q * E, (q + 1) * E)
            total = both(dot(flat_b[0:used], select[:, cols]), full)
            volumes.pop()()
            difference = both(dot(flat_b[0:used], select[:, IF + q * E : IF + (q + 1) * E]), full)
            volumes.pop()()
            term = mix_terms(difference, total, full) * weight[...].reshape(1, IF)[:, cols]
            store_parts(term_b, term, 0, cols, full)
            volumes.pop()()

        if not full:
            pl.when(step == ITERS - 1)(early_products)
        def side_terms(pair):
            diffs, totals = [], []
            for s in (2 * pair, 2 * pair + 1):
                side_copy(step, s ^ 1).wait_recv()
                mine = sends[step, s]
                other = recvs[step, s] * has[s]
                diffs.append(mine - other)
                totals.append(mine + other if s % 2 == 1 else -(mine + other))
            pad = jnp.zeros((ROWS - SEND, 2 * FS), F32)
            difference = jnp.concatenate([jnp.concatenate(diffs, axis=1), pad], axis=0)
            total = jnp.concatenate([jnp.concatenate(totals, axis=1), pad], axis=0)
            term = mix_terms(difference, total, full)
            start = IF + pair * 2 * FS
            store_parts(term_b, term, 0, slice(start, start + 2 * FS), full)

        def scattered(f, start, stop):
            return both(
                dot_t(term_b[0:used, start:stop], select[f * E : (f + 1) * E, IF + start : IF + stop]),
                full,
            )

        side_terms(0)
        for f in range(NF):
            gathered[:, f * E : (f + 1) * E] = scattered(f, 0, IF + 2 * FS)
        side_terms(1)
        for f in range(NF):
            t = gathered[:, f * E : (f + 1) * E] + scattered(f, IF + 2 * FS, IF + 4 * FS)
            for b in range(NV):
                faces[b, f * 24 : (f + 1) * 24, :] = t[b * 24 : (b + 1) * 24]
                faces[b, 144 + f : 145 + f, :] = t[144 + b : 145 + b]
        for b in range(NV):
            hi, lo = split(faces[b])
            if full:
                t = dot(lift_mat[...], jnp.concatenate([hi, lo], axis=0))
            else:
                t = dot(lift_mat[:, 0:ROWS], hi)
            us[step + 1, b] = (us[step + 1, b] + t) * active[...] - SHIFT * us[step, b]
        for s in range(4):
            side_copy(step, s).wait_send()
        return carry

    lax.fori_loop(0, FULL_STEPS, functools.partial(one_step, True), 0)
    lax.fori_loop(FULL_STEPS, ITERS, functools.partial(one_step, False), 0)

    pairs = [(i, j) for i in range(ITERS + 1) for j in range(i, ITERS + 1)]

    def last_products(c, accs):
        accs = list(accs)
        base = pl.multiple_of(c * 8, 8)
        for b in range(NV):
            for lt in range(2):
                lanes = slice(lt * 128, (lt + 1) * 128)
                v = us[ITERS, b, pl.ds(base, 8), lanes]
                for k in range(ITERS):
                    accs[k] = accs[k] + v * us[k, b, pl.ds(base, 8), lanes]
                accs[ITERS] = accs[ITERS] + v * v
        return tuple(accs)

    zero = jnp.zeros((8, 128), F32)
    last = lax.fori_loop(0, 16, last_products, (zero,) * (ITERS + 1))
    accs = [last[i] if j == ITERS else prods[early.index((i, j))] for i, j in pairs]
    rows = [jnp.sum(x, axis=0, keepdims=True) for x in accs]
    rows.append(jnp.zeros((1, 128), F32))
    x = jnp.concatenate(rows, axis=0)
    for amount in (64, 32, 16, 8):
        x = x + pltpu.roll(x, amount, 1)
    row = lax.broadcasted_iota(jnp.int32, (16, 128), 0)
    lane = lax.broadcasted_iota(jnp.int32, (16, 128), 1)
    x = jnp.sum(jnp.where((lane >= row * 8) & (lane < row * 8 + 8), x, 0.0), axis=0, keepdims=True)
    gram[0] = x

    def sum_copy(k, i):
        return pltpu.make_async_remote_copy(
            src_ref=gram.at[k],
            dst_ref=sums_in.at[k, i],
            send_sem=sum_send.at[k, i],
            recv_sem=sum_recv.at[k, i],
            device_id=partner(k, i),
            device_id_type=MESH,
        )

    total = gram[0]
    for k, (_, _, size) in enumerate(STAGES):
        if k > 0:
            gram[k] = total
        for i in range(1, size):
            sum_copy(k, i).start()
        for i in range(1, size):
            sum_copy(k, i).wait_recv()
            total = total + sums_in[k, i]
    for amount in (4, 2, 1):
        total = total + pltpu.roll(total, 128 - amount, 1)

    g = {}
    for n, (i, j) in enumerate(pairs):
        g[i, j] = g[j, i] = jnp.broadcast_to(total[:, 8 * n : 8 * n + 1], (8, 128))
    half = [[SHIFT * g[i, j] + g[i, j + 1] for j in range(ITERS)] for i in range(ITERS + 1)]
    normal = [
        [SHIFT * half[i][j] + half[i + 1][j] for j in range(ITERS)] for i in range(ITERS)
    ]
    rhs = [half[0][j] for j in range(ITERS)]
    low = [[None] * ITERS for _ in range(ITERS)]
    pivot, inv = [], []
    for j in range(ITERS):
        d = normal[j][j]
        for k in range(j):
            d = d - low[j][k] * low[j][k] * pivot[k]
        pivot.append(d)
        usable = d > 1e-6 * normal[j][j]
        inv.append(jnp.where(usable, 1.0 / jnp.where(usable, d, 1.0), 0.0))
        for i in range(j + 1, ITERS):
            v = normal[i][j]
            for k in range(j):
                v = v - low[i][k] * low[j][k] * pivot[k]
            low[i][j] = v * inv[j]
    y = []
    for i in range(ITERS):
        v = rhs[i]
        for k in range(i):
            v = v - low[i][k] * y[k]
        y.append(v)
    coeffs = [y[i] * inv[i] for i in range(ITERS)]
    for i in reversed(range(ITERS)):
        for k in range(i + 1, ITERS):
            coeffs[i] = coeffs[i] - low[k][i] * coeffs[k]
    for b in range(NV):
        for lt in range(2):
            lanes = slice(lt * 128, (lt + 1) * 128)
            x = coeffs[0][0:1] * zs[0, b, 0:125, lanes]
            for k in range(1, ITERS):
                x = x + coeffs[k][0:1] * zs[k, b, 0:125, lanes]
            out[b, :, lanes] = x
    for k, i in partners:
        sum_copy(k, i).wait_send()


def local(n_span, n_chord, *args):
    args = tuple(pltpu.with_memory_space_constraint(a, pltpu.HBM) for a in args + constants())
    held = [(pltpu.SMEM if k in (5, 6) else pltpu.VMEM)(a.shape, a.dtype) for k, a in enumerate(args)]
    return pl.pallas_call(
        functools.partial(kernel, n_span, n_chord),
        out_shape=jax.ShapeDtypeStruct((NV, 125, E), F32),
        in_specs=[pl.BlockSpec(memory_space=pltpu.HBM)] * len(args),
        out_specs=pl.BlockSpec(memory_space=pltpu.VMEM),
        scratch_shapes=held
        + [
            pltpu.SemaphoreType.DMA((len(args),)),
            pltpu.VMEM((ROWS + 384, 256), BF),
            pltpu.VMEM((128, 2 * ROWS), BF),
            pltpu.VMEM((128, E), F32),
            pltpu.VMEM((3, NV, NV, E), F32),
            pltpu.VMEM((COLS, SLOTS), BF),
            pltpu.VMEM((ROWS, 6 * ROWS), BF),
            pltpu.VMEM((ITERS + 1, NV, 128, E), F32),
            pltpu.VMEM((ITERS, NV, 128, E), F32),
            pltpu.VMEM((NV, 256, E), BF),
            pltpu.VMEM((NV, 384, E), F32),
            pltpu.VMEM((ROWS, COLS), F32),
            pltpu.VMEM((2 * ROWS, COLS), BF),
            pltpu.VMEM((6 * ROWS, E), BF),
            pltpu.VMEM((2 * ROWS, IF + 4 * FS), BF),
            pltpu.VMEM((ROWS, COLS), F32),
            pltpu.VMEM((NV, ROWS, E), F32),
            pltpu.VMEM((ITERS, 4, SEND, FS), F32),
            pltpu.VMEM((ITERS, 4, SEND, FS), F32),
            pltpu.VMEM((len(STAGES), 1, 128), F32),
            pltpu.VMEM((len(STAGES), 16, 1, 128), F32),
            pltpu.SemaphoreType.DMA((ITERS, 4)),
            pltpu.SemaphoreType.DMA((ITERS, 4)),
            pltpu.SemaphoreType.DMA((len(STAGES), 16)),
            pltpu.SemaphoreType.DMA((len(STAGES), 16)),
            pltpu.VMEM((ITERS * (ITERS + 1) // 2, 8, 128), F32),
        ],
        compiler_params=pltpu.CompilerParams(
            collective_id=0, has_side_effects=True, vmem_limit_bytes=44 * 1024 * 1024
        ),
    )(*args)


def solution(mesh):
    placed = (
        P(None, None, ("span", "chord")),
        P(("span", "chord")),
        P(("span", "chord")),
        P(None, None, None, ("span", "chord")),
        P(None, None, ("span", "chord")),
        P(),
        P(),
        P(("span", "chord")),
        P(None, ("span", "chord")),
        P(None, ("span", "chord")),
        P(None, ("span", "chord")),
        P(None, ("span", "chord")),
    )
    return jax.shard_map(
        functools.partial(local, mesh.shape["span"], mesh.shape["chord"]),
        mesh=mesh,
        in_specs=placed,
        out_specs=P(None, None, ("span", "chord")),
        check_vma=False,
    )
```

```python
import functools

import jax
import jax.numpy as jnp
import numpy as np
from jax import lax
from jax.experimental import pallas as pl
from jax.experimental.pallas import tpu as pltpu
from jax.sharding import PartitionSpec as P

ITERS = 4
NV = 6
E = 256
IF = 512
FS = 128
NF = 6
ROWS = 160
SEND = 152
COLS = NF * E
SLOTS = 2 * IF + 4 * FS
SHIFT = 1.5
FULL_STEPS = 2
LOAD_ORDER = (8, 9, 10, 11, 0, 1, 4, 12, 3, 5, 6, 7, 2, 13)
STAGES = (("span", 1, 8), ("chord", 1, 16))
MESH = pl.DeviceIdType.MESH
BF = jnp.bfloat16
F32 = jnp.float32


def face_row(face, t):
    return face * 24 + t if t < 24 else 144 + face


def constants():
    mode_mat = np.zeros((ROWS + 384, 128), np.float32)
    lift = np.zeros((128, ROWS), np.float32)
    sign = [1.0, -1.0, 1.0, -1.0, 1.0]
    for i in range(5):
        for j in range(5):
            for k in range(5):
                m = 25 * i + 5 * j + k
                idx = (i, j, k)
                rest = (5 * j + k, 5 * i + k, 5 * i + j)
                step = (25, 5, 1)
                for d in range(3):
                    for end in range(2):
                        r = face_row(2 * d + end, rest[d])
                        value = 0.5 * (sign[idx[d]] if end == 0 else 1.0)
                        mode_mat[r, m] = value
                        lift[m, r] = value
                    for low in range(idx[d]):
                        if (idx[d] - low) % 2 == 1:
                            out = m - step[d] * (idx[d] - low)
                            mode_mat[ROWS + 128 * d + out, m] = 2 * low + 1
    return (
        jnp.asarray(mode_mat),
        jnp.asarray(np.concatenate([lift, lift], axis=1)),
    )


def split(x):
    hi = x.astype(BF)
    return hi, (x - hi.astype(F32)).astype(BF)


def dot(a, b):
    return jnp.dot(a, b, preferred_element_type=F32)


def dot_t(a, b):
    return lax.dot_general(a, b, (((1,), (1,)), ((), ())), preferred_element_type=F32)


def kernel(
    n_span,
    n_chord,
    *refs,
):
    operands, out, refs = refs[:14], refs[14], refs[15:]
    held, load_sem, refs = refs[:14], refs[14], refs[15:]
    (
        src,
        degrees,
        time_shift,
        jac,
        binv,
        diss,
        conv,
        weight,
        face_el,
        face_no,
        side_el,
        side_no,
        mode_in,
        lift_in,
    ) = held
    (
        mode_mat,
        lift_mat,
        active,
        jac2,
        select,
        mix,
        us,
        zs,
        modes,
        grads,
        flat,
        flat_b,
        uv_b,
        term_b,
        gathered,
        faces,
        sends,
        recvs,
        gram,
        sums_in,
        send_sem,
        recv_sem,
        sum_send,
        sum_recv,
        prods,
    ) = refs
    loads = [pltpu.make_async_copy(a, b, load_sem.at[k]) for k, (a, b) in enumerate(zip(operands, held))]
    for k in LOAD_ORDER:
        loads[k].start()

    def arrived(*which):
        for k in which:
            loads[k].wait()

    span = lax.axis_index("span")
    chord = lax.axis_index("chord")

    barrier = pltpu.get_barrier_semaphore()
    def partner(stage, i):
        axis, stride, size = STAGES[stage]
        index = span if axis == "span" else chord
        digit = lax.rem(index // stride, size)
        index = index + (lax.rem(digit + i, size) - digit) * stride
        return (index, chord) if axis == "span" else (span, index)

    partners = [(k, i) for k, stage in enumerate(STAGES) for i in range(1, stage[2])]
    for k, i in partners:
        pl.semaphore_signal(barrier, inc=1, device_id=partner(k, i), device_id_type=MESH)

    has = (span > 0, span < n_span - 1, chord > 0, chord < n_chord - 1)
    has = [h.astype(F32) for h in has]
    targets = (
        (lax.rem(span + n_span - 1, n_span), chord),
        (lax.rem(span + 1, n_span), chord),
        (span, lax.rem(chord + n_chord - 1, n_chord)),
        (span, lax.rem(chord + 1, n_chord)),
    )

    arrived(8, 9, 10, 11)
    cols_in = face_no[...] * E + face_el[...]
    cols_sd = side_no[...] * E + side_el[...]
    left = cols_in[0:1, :]
    right = cols_in[1:2, :]
    row16 = lax.broadcasted_iota(jnp.int32, (16, FS), 0)

    def build(c, carry):
        base = pl.multiple_of(c * 16, 16)
        rows = row16 + base
        for q in range(4):
            l = (rows == left[:, q * FS : (q + 1) * FS]).astype(F32)
            r = (rows == right[:, q * FS : (q + 1) * FS]).astype(F32)
            s = (rows == cols_sd[q : q + 1, :]).astype(F32)
            select[pl.ds(base, 16), IF + q * FS : IF + (q + 1) * FS] = (l - r).astype(BF)
            select[pl.ds(base, 16), q * FS : (q + 1) * FS] = (l + r).astype(BF)
            select[pl.ds(base, 16), 2 * IF + q * FS : 2 * IF + (q + 1) * FS] = s.astype(BF)
        return carry

    lax.fori_loop(0, COLS // 16, build, 0, unroll=4)

    arrived(0, 1, 3, 5, 6)
    mode = lax.broadcasted_iota(jnp.int32, (128, 128), 0)

    def digit(x, unit):
        return sum((x >= unit * k).astype(jnp.int32) for k in range(1, 5))

    first = digit(mode, 25)
    second = digit(mode - 25 * first, 5)
    third = mode - 25 * first - 5 * second
    highest = jnp.maximum(jnp.maximum(first, second), third)
    highest = jnp.where(mode < 125, highest, 99)
    for lt in range(2):
        lanes = slice(lt * 128, (lt + 1) * 128)
        act = (highest <= degrees[...].reshape(1, E)[:, lanes]).astype(F32)
        active[:, lanes] = act
        for b in range(NV):
            us[0, b, 125:128, lanes] = jnp.zeros((3, 128), F32)
            us[0, b, 0:125, lanes] = src[b, :, lanes] * act[0:125]
    jac2[...] = jac[...] * 0.2

    r24 = lax.broadcasted_iota(jnp.int32, (24, ROWS), 0)
    c24 = lax.broadcasted_iota(jnp.int32, (24, ROWS), 1)
    r16 = lax.broadcasted_iota(jnp.int32, (16, ROWS), 0)
    c16 = lax.broadcasted_iota(jnp.int32, (16, ROWS), 1)
    mixed = []
    for mat in (diss, conv):
        parts = []
        for x in range(NV):
            acc = jnp.zeros((24, ROWS), F32)
            for y in range(NV):
                acc = acc + jnp.where(c24 == r24 + y * 24, mat[x, y], 0.0)
            parts.append(acc)
        acc = jnp.zeros((16, ROWS), F32)
        for x in range(NV):
            for y in range(NV):
                acc = acc + jnp.where((r16 == x) & (c16 == 144 + y), mat[x, y], 0.0)
        parts.append(acc)
        mixed.append(jnp.concatenate(parts, axis=0))
    mixed = jnp.concatenate(mixed, axis=1)
    mix_hi, mix_lo = split(mixed)
    mix[:, 0 : 2 * ROWS] = mix_hi
    mix[:, 2 * ROWS : 4 * ROWS] = mix_hi
    mix[:, 4 * ROWS : 6 * ROWS] = mix_lo

    flat[...] = jnp.zeros_like(flat)
    faces[...] = jnp.zeros_like(faces)
    arrived(2, 4, 7, 12, 13)
    mode_mat[:, 0:128] = mode_in[...].astype(BF)
    mode_mat[:, 128:256] = mode_in[...].astype(BF)
    lift_mat[...] = lift_in[...].astype(BF)
    pl.semaphore_wait(barrier, len(partners))

    def side_copy(step, s):
        return pltpu.make_async_remote_copy(
            src_ref=sends.at[step, s],
            dst_ref=recvs.at[step, s ^ 1],
            send_sem=send_sem.at[step, s],
            recv_sem=recv_sem.at[step, s ^ 1],
            device_id=targets[s],
            device_id_type=MESH,
        )

    def mix_terms(difference, total, full):
        d_hi, d_lo = split(difference)
        t_hi, t_lo = split(total)
        parts = (d_hi, t_hi, d_lo, t_lo, d_hi, t_hi) if full else (d_hi, t_hi)
        for k, part in enumerate(parts):
            uv_b[k * ROWS : (k + 1) * ROWS, :] = part
        return dot(mix[:, 0 : len(parts) * ROWS], uv_b[0 : len(parts) * ROWS, :])

    def store_parts(ref, x, row, cols, full):
        hi, lo = split(x)
        n = x.shape[0]
        ref[row : row + n, cols] = hi
        if full:
            ref[ROWS + row : ROWS + row + n, cols] = lo

    def both(t, full):
        return t[0:ROWS] + t[ROWS:] if full else t

    early = [(i, j) for i in range(ITERS) for j in range(i, ITERS)]

    def early_products():
        def products(c, accs):
            accs = list(accs)
            base = pl.multiple_of(c * 8, 8)
            for b in range(NV):
                for lt in range(2):
                    lanes = slice(lt * 128, (lt + 1) * 128)
                    v = [us[k, b, pl.ds(base, 8), lanes] for k in range(ITERS)]
                    for n, (i, j) in enumerate(early):
                        accs[n] = accs[n] + v[i] * v[j]
            return tuple(accs)

        accs = lax.fori_loop(0, 16, products, (jnp.zeros((8, 128), F32),) * len(early))
        for n, acc in enumerate(accs):
            prods[n] = acc

    def one_step(full, step, carry):
        used = 2 * ROWS if full else ROWS
        for a0 in range(0, NV, 2):
            for lt in range(2):
                lanes = slice(lt * 128, (lt + 1) * 128)
                acc = [None, None]
                for b in range(NV):
                    u = us[step, b, :, lanes]
                    for p in range(2):
                        t = binv[a0 + p, b : b + 1, lanes] * u
                        acc[p] = t if acc[p] is None else acc[p] + t
                for p in range(2):
                    zs[step, a0 + p, :, lanes] = acc[p]
                    hi, lo = split(acc[p])
                    modes[a0 + p, 0:128, lanes] = hi
                    modes[a0 + p, 128:256, lanes] = lo
            for b in (a0, a0 + 1):
                t = dot(mode_mat[0:ROWS, :], modes[b])
                for f in range(NF):
                    cols = slice(f * E, (f + 1) * E)
                    flat[b * 24 : (b + 1) * 24, cols] = t[f * 24 : (f + 1) * 24]
                    flat[144 + b : 145 + b, cols] = t[144 + f : 145 + f]
            store_parts(flat_b, flat[a0 * 24 : (a0 + 2) * 24, :], a0 * 24, slice(0, COLS), full)
        store_parts(flat_b, flat[144:ROWS, :], 144, slice(0, COLS), full)
        for pair in (1, 0):
            cols = slice(2 * IF + pair * 2 * FS, 2 * IF + (pair + 1) * 2 * FS)
            t = both(dot(flat_b[0:used], select[:, cols]), full)
            for s in (2 * pair, 2 * pair + 1):
                sends[step, s] = t[0:SEND, (s % 2) * FS : (s % 2 + 1) * FS]
                side_copy(step, s).start()

        for b in range(NV):
            grads[b] = dot(mode_mat[ROWS:, :], modes[b])
        def volume(a0, lt):
            lanes = slice(lt * 128, (lt + 1) * 128)
            shift = time_shift[...].reshape(1, E)[:, lanes]
            acc = [shift * zs[step, a0 + p, :, lanes] for p in range(2)]
            for d in range(3):
                for b in range(NV):
                    g = grads[b, d * 128 : (d + 1) * 128, lanes]
                    for p in range(2):
                        acc[p] = acc[p] + jac2[d, a0 + p, b : b + 1, lanes] * g
            for p in range(2):
                us[step + 1, a0 + p, :, lanes] = acc[p]

        volumes = [functools.partial(volume, a0, lt) for lt in range(2) for a0 in range(0, NV, 2)]

        for q in range(2):
            cols = slice(q * E, (q + 1) * E)
            total = both(dot(flat_b[0:used], select[:, cols]), full)
            volumes.pop()()
            difference = both(dot(flat_b[0:used], select[:, IF + q * E : IF + (q + 1) * E]), full)
            volumes.pop()()
            term = mix_terms(difference, total, full) * weight[...].reshape(1, IF)[:, cols]
            store_parts(term_b, term, 0, cols, full)
            volumes.pop()()

        if not full:
            pl.when(step == ITERS - 1)(early_products)
        def side_terms(pair):
            diffs, totals = [], []
            for s in (2 * pair, 2 * pair + 1):
                side_copy(step, s ^ 1).wait_recv()
                mine = sends[step, s]
                other = recvs[step, s] * has[s]
                diffs.append(mine - other)
                totals.append(mine + other if s % 2 == 1 else -(mine + other))
            pad = jnp.zeros((ROWS - SEND, 2 * FS), F32)
            difference = jnp.concatenate([jnp.concatenate(diffs, axis=1), pad], axis=0)
            total = jnp.concatenate([jnp.concatenate(totals, axis=1), pad], axis=0)
            term = mix_terms(difference, total, full)
            start = IF + pair * 2 * FS
            store_parts(term_b, term, 0, slice(start, start + 2 * FS), full)

        def scattered(f, start, stop):
            return both(
                dot_t(term_b[0:used, start:stop], select[f * E : (f + 1) * E, IF + start : IF + stop]),
                full,
            )

        side_terms(0)
        for f in range(NF):
            gathered[:, f * E : (f + 1) * E] = scattered(f, 0, IF + 2 * FS)
        side_terms(1)
        for f in range(NF):
            t = gathered[:, f * E : (f + 1) * E] + scattered(f, IF + 2 * FS, IF + 4 * FS)
            for b in range(NV):
                faces[b, f * 24 : (f + 1) * 24, :] = t[b * 24 : (b + 1) * 24]
                faces[b, 144 + f : 145 + f, :] = t[144 + b : 145 + b]
        for b in range(NV):
            hi, lo = split(faces[b])
            if full:
                t = dot(lift_mat[...], jnp.concatenate([hi, lo], axis=0))
            else:
                t = dot(lift_mat[:, 0:ROWS], hi)
            us[step + 1, b] = (us[step + 1, b] + t) * active[...] - SHIFT * us[step, b]
        return carry

    lax.fori_loop(0, FULL_STEPS, functools.partial(one_step, True), 0)
    lax.fori_loop(FULL_STEPS, ITERS, functools.partial(one_step, False), 0)

    pairs = [(i, j) for i in range(ITERS + 1) for j in range(i, ITERS + 1)]

    def last_products(c, accs):
        accs = list(accs)
        base = pl.multiple_of(c * 8, 8)
        for b in range(NV):
            for lt in range(2):
                lanes = slice(lt * 128, (lt + 1) * 128)
                v = us[ITERS, b, pl.ds(base, 8), lanes]
                for k in range(ITERS):
                    accs[k] = accs[k] + v * us[k, b, pl.ds(base, 8), lanes]
                accs[ITERS] = accs[ITERS] + v * v
        return tuple(accs)

    zero = jnp.zeros((8, 128), F32)
    last = lax.fori_loop(0, 16, last_products, (zero,) * (ITERS + 1))
    accs = [last[i] if j == ITERS else prods[early.index((i, j))] for i, j in pairs]
    rows = [jnp.sum(x, axis=0, keepdims=True) for x in accs]
    rows.append(jnp.zeros((1, 128), F32))
    x = jnp.concatenate(rows, axis=0)
    for amount in (64, 32, 16, 8):
        x = x + pltpu.roll(x, amount, 1)
    row = lax.broadcasted_iota(jnp.int32, (16, 128), 0)
    lane = lax.broadcasted_iota(jnp.int32, (16, 128), 1)
    x = jnp.sum(jnp.where((lane >= row * 8) & (lane < row * 8 + 8), x, 0.0), axis=0, keepdims=True)
    gram[0] = x

    def sum_copy(k, i):
        return pltpu.make_async_remote_copy(
            src_ref=gram.at[k],
            dst_ref=sums_in.at[k, i],
            send_sem=sum_send.at[k, i],
            recv_sem=sum_recv.at[k, i],
            device_id=partner(k, i),
            device_id_type=MESH,
        )

    total = gram[0]
    for k, (_, _, size) in enumerate(STAGES):
        if k > 0:
            gram[k] = total
        for i in range(1, size):
            sum_copy(k, i).start()
        for i in range(1, size):
            sum_copy(k, i).wait_recv()
            total = total + sums_in[k, i]
    for amount in (4, 2, 1):
        total = total + pltpu.roll(total, 128 - amount, 1)

    g = {}
    for n, (i, j) in enumerate(pairs):
        g[i, j] = g[j, i] = jnp.broadcast_to(total[:, 8 * n : 8 * n + 1], (8, 128))
    half = [[SHIFT * g[i, j] + g[i, j + 1] for j in range(ITERS)] for i in range(ITERS + 1)]
    normal = [
        [SHIFT * half[i][j] + half[i + 1][j] for j in range(ITERS)] for i in range(ITERS)
    ]
    rhs = [half[0][j] for j in range(ITERS)]
    low = [[None] * ITERS for _ in range(ITERS)]
    pivot, inv = [], []
    for j in range(ITERS):
        d = normal[j][j]
        for k in range(j):
            d = d - low[j][k] * low[j][k] * pivot[k]
        pivot.append(d)
        usable = d > 1e-6 * normal[j][j]
        inv.append(jnp.where(usable, 1.0 / jnp.where(usable, d, 1.0), 0.0))
        for i in range(j + 1, ITERS):
            v = normal[i][j]
            for k in range(j):
                v = v - low[i][k] * low[j][k] * pivot[k]
            low[i][j] = v * inv[j]
    y = []
    for i in range(ITERS):
        v = rhs[i]
        for k in range(i):
            v = v - low[i][k] * y[k]
        y.append(v)
    coeffs = [y[i] * inv[i] for i in range(ITERS)]
    for i in reversed(range(ITERS)):
        for k in range(i + 1, ITERS):
            coeffs[i] = coeffs[i] - low[k][i] * coeffs[k]
    for b in range(NV):
        for lt in range(2):
            lanes = slice(lt * 128, (lt + 1) * 128)
            x = coeffs[0][0:1] * zs[0, b, 0:125, lanes]
            for k in range(1, ITERS):
                x = x + coeffs[k][0:1] * zs[k, b, 0:125, lanes]
            out[b, :, lanes] = x
    for k, i in partners:
        sum_copy(k, i).wait_send()
    for step in range(ITERS):
        for s in range(4):
            side_copy(step, s).wait_send()


def local(n_span, n_chord, *args):
    args = tuple(pltpu.with_memory_space_constraint(a, pltpu.HBM) for a in args + constants())
    held = [(pltpu.SMEM if k in (5, 6) else pltpu.VMEM)(a.shape, a.dtype) for k, a in enumerate(args)]
    return pl.pallas_call(
        functools.partial(kernel, n_span, n_chord),
        out_shape=jax.ShapeDtypeStruct((NV, 125, E), F32),
        in_specs=[pl.BlockSpec(memory_space=pltpu.HBM)] * len(args),
        out_specs=pl.BlockSpec(memory_space=pltpu.VMEM),
        scratch_shapes=held
        + [
            pltpu.SemaphoreType.DMA((len(args),)),
            pltpu.VMEM((ROWS + 384, 256), BF),
            pltpu.VMEM((128, 2 * ROWS), BF),
            pltpu.VMEM((128, E), F32),
            pltpu.VMEM((3, NV, NV, E), F32),
            pltpu.VMEM((COLS, SLOTS), BF),
            pltpu.VMEM((ROWS, 6 * ROWS), BF),
            pltpu.VMEM((ITERS + 1, NV, 128, E), F32),
            pltpu.VMEM((ITERS, NV, 128, E), F32),
            pltpu.VMEM((NV, 256, E), BF),
            pltpu.VMEM((NV, 384, E), F32),
            pltpu.VMEM((ROWS, COLS), F32),
            pltpu.VMEM((2 * ROWS, COLS), BF),
            pltpu.VMEM((6 * ROWS, E), BF),
            pltpu.VMEM((2 * ROWS, IF + 4 * FS), BF),
            pltpu.VMEM((ROWS, COLS), F32),
            pltpu.VMEM((NV, ROWS, E), F32),
            pltpu.VMEM((ITERS, 4, SEND, FS), F32),
            pltpu.VMEM((ITERS, 4, SEND, FS), F32),
            pltpu.VMEM((len(STAGES), 1, 128), F32),
            pltpu.VMEM((len(STAGES), 16, 1, 128), F32),
            pltpu.SemaphoreType.DMA((ITERS, 4)),
            pltpu.SemaphoreType.DMA((ITERS, 4)),
            pltpu.SemaphoreType.DMA((len(STAGES), 16)),
            pltpu.SemaphoreType.DMA((len(STAGES), 16)),
            pltpu.VMEM((ITERS * (ITERS + 1) // 2, 8, 128), F32),
        ],
        compiler_params=pltpu.CompilerParams(
            collective_id=0, has_side_effects=True, vmem_limit_bytes=44 * 1024 * 1024
        ),
    )(*args)


def solution(mesh):
    placed = (
        P(None, None, ("span", "chord")),
        P(("span", "chord")),
        P(("span", "chord")),
        P(None, None, None, ("span", "chord")),
        P(None, None, ("span", "chord")),
        P(),
        P(),
        P(("span", "chord")),
        P(None, ("span", "chord")),
        P(None, ("span", "chord")),
        P(None, ("span", "chord")),
        P(None, ("span", "chord")),
    )
    return jax.shard_map(
        functools.partial(local, mesh.shape["span"], mesh.shape["chord"]),
        mesh=mesh,
        in_specs=placed,
        out_specs=P(None, None, ("span", "chord")),
        check_vma=False,
    )
```
